512 devices in a mesh: section: 16 (over x, z_hi, core), fsdp: 32 (over y, z_lo).
Axes of the slice: x: 4, y: 8, z: 8 (z_hi: 2, z_lo: 4; z = z_hi * 4 + z_lo), core: 2. Of those that a mesh axis runs over, the one named last changes fastest.
Arguments:
- inputs: bfloat16 [4, 32, 32, 2048], P(None, 'fsdp', 'section'), may hold values from -6 to 6
- segments: int32 [4, 32, 32], P(None, 'fsdp', 'section'), may hold values from 0 to 7, never falling along the last dimension, each value on 1 to 16 neighbouring positions
- norm_gains: bfloat16 [16, 2048], P('section', 'fsdp'), may hold values from 0.099609375 to 1.8984375
- w_query: bfloat16 [16, 2048, 1024], P('section', 'fsdp'), may hold values from -0.125 to 0.125
- w_keyval: bfloat16 [16, 2048, 512], P('section', 'fsdp'), may hold values from -0.125 to 0.125
- w_output: bfloat16 [16, 1024, 2048], P('section', 'fsdp'), may hold values from -0.1875 to 0.1875
Outputs:
- hidden: bfloat16 [4, 32, 32, 2048], P(None, 'fsdp', 'section')
The draws below stay inside these ranges and needn't reach their ends.
Inputs may be any that keep to these rules, and one draw needn't show every extreme that they name: `segments`: within each sequence the numbers never fall, each document spans at most 16 positions, and some document spans exactly that many.
All inputs are finite; a program needn't handle non-finite values.
Results may differ from the reference program's by a relative error of at most 0.034.
Values may be sent and summed in bfloat16 or wider, within the bound.
A program may use at most 64 MiB of HBM per device.

```python
import math
import jax
import jax.numpy as jnp
import numpy as np
from jax import lax

D = 2048
HEAD = 64
HEADS = 16
KV_HEADS = 4
SEQ = 32
MICRO = 4
LAYERS = 16
SEQS = 32
QW = 1024
KVW = 512


def levels(own_key, shape, cuts, least, top_value):
    def one(dim, parts):
        draws = jax.random.uniform(jax.random.fold_in(jax.random.fold_in(own_key, 6), dim), (parts,), jnp.float32, least / len(cuts), top_value / len(cuts))
        return jnp.repeat(jnp.exp(draws), shape[dim] // parts).reshape((-1,) + (1,) * (len(shape) - dim - 1))

    level = one(*cuts[0])
    for cut in cuts[1:]:
        level = level * one(*cut)
    return level


def profile(number_of, total, bound, lean):
    loads = [(1 << 20) // math.isqrt(rank ** lean) + 1 for rank in range(2, number_of + 1)]
    spare, given = total - bound - (number_of - 1), [1] * (number_of - 1)
    while spare > 0:
        free = [i for i in range(number_of - 1) if given[i] < bound]
        mass, budget = sum([loads[i] for i in free]), spare
        for i in free:
            extra = min(bound - given[i], max(1, budget * loads[i] // mass), spare)
            given[i] = given[i] + extra
            spare = spare - extra
    return np.array([bound] + given)


def ragged(own_key, count, total, reach, slope):
    if count == 2:
        one = jax.random.randint(own_key, (), max(1, total - reach), min(reach, total - 1) + 1)
        return jnp.stack([one, total - one])
    lengths = jnp.asarray(profile(count, total, reach, slope), jnp.int32)
    twos = (count - 1) // 2
    giver, sink = lengths[1:1 + 2 * twos:2], lengths[2:2 + 2 * twos:2]
    room = jnp.minimum(giver - 1, reach - sink)
    shifted = jax.random.randint(jax.random.fold_in(own_key, 1), (twos,), 0, 1 << 20) % (room + 1)
    lengths = lengths.at[1:1 + 2 * twos:2].set(giver - shifted).at[2:2 + 2 * twos:2].set(sink + shifted)
    return lengths[jax.random.permutation(jax.random.fold_in(own_key, 2), count)]


def centred(stream_key, shape, spread, limit, cuts=(), kind=jnp.bfloat16):
    entries = jax.random.normal(stream_key, shape, jnp.float32) * spread
    if len(cuts) > 0:
        entries = levels(stream_key, shape, cuts, -0.22, 0.18) * entries
    return jnp.clip(entries, min=-limit, max=limit).astype(kind)


def setup_inputs(seed: int = 0) -> dict:
    splits = jax.random.split(jax.random.key(seed), 7)
    return {
        "inputs": centred(splits[0], (MICRO, SEQS, SEQ, D), 1.0, 6.0, ((1, 32), (2, 16))),
        "segments": jax.vmap(lambda own: jnp.searchsorted(jnp.cumsum(ragged(own, SEQ // 4, SEQ, SEQ // 2, 2)), jnp.arange(SEQ), side="right"))(jax.random.split(splits[1], MICRO * SEQS)).reshape((MICRO, SEQS, SEQ)).astype(jnp.int32),
        "norm_gains": jnp.clip(1.0 + 0.18 * jax.random.normal(splits[2], (LAYERS, D), jnp.float32), 0.099609375, 1.8984375).astype(jnp.bfloat16),
        "w_query": centred(splits[3], (LAYERS, D, QW), D ** -0.5, 0.125, ((0, 16), (1, 32))),
        "w_keyval": centred(splits[4], (LAYERS, D, KVW), D ** -0.5, 0.125, ((0, 16), (1, 32))),
        "w_output": centred(splits[5], (LAYERS, QW, D), QW ** -0.5, 0.1875, ((0, 16), (1, 32))),
    }


EPSILON = 1e-05
THETA = 500000.0

def rope_tables(seq_len, size):
    position = jnp.arange(seq_len, dtype=jnp.float32)
    freq = THETA ** (-jnp.arange(size // 2, dtype=jnp.float32) * 2.0 / size)
    angle = position[:, None] * freq[None, :]
    return (jnp.cos(angle), jnp.sin(angle))

def rotate(values, cosine, sine_table):
    half_size = values.shape[-1] // 2
    lower_half = values[..., :half_size]
    upper_half = values[..., half_size:]
    cos_part = cosine[:, None, :]
    sin_part = sine_table[:, None, :]
    return jnp.concatenate([lower_half * cos_part - upper_half * sin_part, upper_half * cos_part + lower_half * sin_part], axis=-1)

def attend_layer(hidden, segment, gain_row, w_query, w_keyval, w_output):
    batch_size, seq_len, model_width = hidden.shape
    hidden_f = hidden.astype(jnp.float32)
    scaled = hidden_f * lax.rsqrt(lax.optimization_barrier(jnp.mean(hidden_f * hidden_f, axis=-1, keepdims=True)) + EPSILON) * gain_row.astype(jnp.float32)
    normed = scaled.astype(jnp.bfloat16).reshape(batch_size * seq_len, model_width)
    queries = jnp.dot(normed, w_query, preferred_element_type=jnp.float32).reshape(batch_size, seq_len, HEADS, HEAD)
    keyval = jnp.dot(normed, w_keyval, preferred_element_type=jnp.float32).reshape(batch_size, seq_len, 2, KV_HEADS, HEAD)
    cosine, sine_table = rope_tables(seq_len, HEAD)
    queries = rotate(queries, cosine, sine_table).astype(jnp.bfloat16)
    key_rows = rotate(keyval[:, :, 0], cosine, sine_table).astype(jnp.bfloat16)
    value_rows = keyval[:, :, 1].astype(jnp.bfloat16)
    queries = queries.reshape(batch_size, seq_len, KV_HEADS, HEADS // KV_HEADS, HEAD)
    scores = jnp.einsum('bskgd,btkd->bkgst', queries.astype(jnp.float32), key_rows.astype(jnp.float32)) * HEAD ** (-0.5)
    position = jnp.arange(seq_len)
    allowed = (position[None, :, None] >= position[None, None, :]) & (segment[:, :, None] == segment[:, None, :])
    exps = jnp.where(allowed[:, None, None], jnp.exp(scores), 0.0)
    weights_bf = (exps / lax.optimization_barrier(jnp.sum(exps, axis=-1, keepdims=True))).astype(jnp.bfloat16)
    attended = jnp.einsum('bkgst,btkd->bskgd', weights_bf.astype(jnp.float32), value_rows.astype(jnp.float32)).astype(jnp.bfloat16)
    update = jnp.dot(attended.reshape(batch_size * seq_len, HEADS * HEAD), w_output, preferred_element_type=jnp.float32)
    return (hidden_f + update.reshape(batch_size, seq_len, model_width)).astype(jnp.bfloat16)

def reference(inputs, segments, norm_gains, w_query, w_keyval, w_output):
    hidden = inputs.reshape(MICRO * SEQS, SEQ, D)
    segment = segments.reshape(MICRO * SEQS, SEQ)
    for layer_index in range(LAYERS):
        hidden = attend_layer(hidden, segment, norm_gains[layer_index], w_query[layer_index], w_keyval[layer_index], w_output[layer_index])
    return hidden.reshape(MICRO, SEQS, SEQ, D)
```

```python
import jax
import jax.numpy as jnp
import numpy as np
from jax import lax
from jax.experimental import pallas as pl
from jax.experimental.pallas import tpu as pltpu
from jax.sharding import PartitionSpec as P

MESH = pl.DeviceIdType.MESH
BF16 = jnp.bfloat16
F32 = jnp.float32
EPSILON = 1e-05
THETA = 500000.0
SEQ = 32
MICRO = 4
WIDTH = 2048
CHUNKS = 4
CHUNK = WIDTH // CHUNKS
QW = 1024
KW = 256
QKV = 1536
LAST = 15


def rope_tables():
    position = np.arange(SEQ, dtype=np.float32)
    freq = (THETA ** (-np.arange(32, dtype=np.float32) * 2.0 / 64)).astype(np.float32)
    angle = (position[:, None] * freq[None, :]).astype(np.float32)
    c, s = np.cos(angle), np.sin(angle)
    return (
        np.concatenate([c, c, c, c], 1).astype(np.float32),
        np.concatenate([-s, s, -s, s], 1).astype(np.float32),
    )


def attention(acc, squares, cosine, sine, mask_t):
    acc = acc * lax.rsqrt(squares * (1.0 / WIDTH) + EPSILON)
    width = QW + KW
    qk = acc[:, :width]
    lane = lax.broadcasted_iota(jnp.int32, (SEQ, width), 1)
    swapped = jnp.where(
        (lane & 63) < 32, pltpu.roll(qk, width - 32, 1), pltpu.roll(qk, 32, 1)
    )
    tiles = width // 128
    qk = (
        qk * jnp.concatenate([cosine] * tiles, axis=1)
        + swapped * jnp.concatenate([sine] * tiles, axis=1)
    ).astype(BF16)
    values = acc[:, width:].astype(BF16)
    outs = []
    for g in range(4):
        key = qk[:, QW + 64 * g : QW + 64 * g + 64]
        value = values[:, 64 * g : 64 * g + 64]
        queries = jnp.concatenate(
            [qk[:, 256 * g + 64 * i : 256 * g + 64 * i + 64] for i in range(4)], axis=0
        )
        scores = lax.dot_general(
            key, queries, (((1,), (1,)), ((), ())), preferred_element_type=F32
        )
        scores = jnp.where(mask_t, scores * 0.125, -1e30)
        exps = jnp.exp(scores - jnp.max(scores, axis=0, keepdims=True))
        probs = (exps / jnp.sum(exps, axis=0, keepdims=True)).astype(BF16)
        mixed = lax.dot_general(
            probs, value, (((0,), (0,)), ((), ())), preferred_element_type=F32
        )
        outs.append(jnp.concatenate([mixed[32 * i : 32 * i + 32] for i in range(4)], axis=1))
    return jnp.concatenate(outs, axis=1).astype(BF16)


def kernel(
    in_ref, wa_ref, wb_ref, cos_ref, sin_ref, out_ref,
    w1, w2, xin, mask, xrecv, xsend, staged, owned,
    z_send, z_recv, ring_send, ring_recv, sib_send, sib_recv,
    in_send, in_recv, mask_send, mask_recv, x_send, x_recv, o_send, o_recv,
):
    section, fsdp = lax.axis_index("section"), lax.axis_index("fsdp")
    x, zhi, core = section // 4, (section // 2) % 2, section % 2
    y, z = fsdp // 4, fsdp % 4
    half = ((z + 1) // 2) % 2
    layer = (2 * x + zhi) * 2 + half
    plane = section - core

    def remote(src, dst, send, recv, to_section, to_fsdp):
        return pltpu.make_async_remote_copy(
            src_ref=src, dst_ref=dst, send_sem=send, recv_sem=recv,
            device_id=(to_section, to_fsdp), device_id_type=MESH,
        )

    def arrived(dst, recv):
        remote(dst, dst, z_send.at[0], recv, plane + 1 - core, fsdp).wait_recv()

    own_positions = xin.at[:, pl.ds(2 * section, 2)]
    in_section, in_fsdp = z % 2, y * 4 + 3 * (z // 2)
    in_self = (section == in_section) & (fsdp == in_fsdp)
    in_remote = remote(in_ref, own_positions, in_send, in_recv, in_section, in_fsdp)
    in_local = pltpu.make_async_copy(in_ref, own_positions, in_recv)

    @pl.when(in_self)
    def _():
        in_local.start()

    @pl.when(jnp.logical_not(in_self))
    def _():
        in_remote.start()

    pair, odd = z // 2, z % 2
    z_copies = []
    for part, (src, full, rows) in enumerate(((wa_ref, w1, 64), (wb_ref, w2, 32))):
        for t in range(2):
            to_z = core if t == 0 else 3 - core
            dst = full.at[y, pair, pl.ds(pl.multiple_of(odd * rows, rows), rows)]
            is_self = (pair == core) & (to_z == z)
            far = remote(
                src, dst, z_send.at[part * 2 + t], z_recv.at[part * 2 + odd],
                plane + pair, y * 4 + to_z,
            )
            near = pltpu.make_async_copy(src, dst, z_recv.at[part * 2 + odd])

            @pl.when(is_self)
            def _(near=near):
                near.start()

            @pl.when(jnp.logical_not(is_self))
            def _(far=far):
                far.start()

            z_copies.append((is_self, far))

    right, left = ((y + 1) % 8) * 4 + z, ((y + 7) % 8) * 4 + z
    sibling = plane + 1 - core
    sends = []
    counts = [0, 0]

    def ring(full, column, rows, direction, step, part):
        ref = full.at[column, core, rows]
        copy = remote(
            ref, ref, ring_send.at[counts[0]], ring_recv.at[(direction * 4 + step) * 2 + part],
            section, right if direction == 0 else left,
        )
        counts[0] += 1
        copy.start()
        sends.append(copy)

    def across(full, column, rows, part):
        ref = full.at[column, core, rows]
        copy = remote(ref, ref, sib_send.at[counts[1]], sib_recv.at[part], sibling, fsdp)
        counts[1] += 1
        copy.start()
        sends.append(copy)

    sizes = ((w1, 64), (w2, 32))
    for part, (full, rows) in enumerate(sizes):
        for u in range(2):
            arrived(full.at[y, core, pl.ds(u * rows, rows)], z_recv.at[part * 2 + u])
        whole = pl.ds(0, 2 * rows)
        for direction in range(2):
            ring(full, y, whole, direction, 0, part)
        across(full, y, whole, part)
    for step in range(1, 5):
        for part, (full, rows) in enumerate(sizes):
            for direction in range(2):
                column = (y + (8 - step if direction == 0 else step)) % 8
                kept = pl.ds(direction * rows, rows)
                whole = pl.ds(0, 2 * rows)
                got = whole if step < 4 else kept
                arrived(
                    full.at[column, core, got],
                    ring_recv.at[(direction * 4 + step - 1) * 2 + part],
                )
                if step < 4:
                    ring(full, column, whole if step < 3 else kept, direction, step, part)
                across(full, column, got, part)
    for part, (full, rows) in enumerate(sizes):
        arrived(full.at[:, 1 - core], sib_recv.at[part])

    first = layer == 0
    last = layer == LAST

    @pl.when(first)
    def _():
        arrived(xin, in_recv)
        row = lax.broadcasted_iota(jnp.int32, (SEQ, 128), 0)
        query = lax.broadcasted_iota(jnp.int32, (SEQ, 128), 1) % SEQ

        def load(m, carry):
            for i in range(16):
                xrecv[m, i // 4, :, (i % 4) * 128 : (i % 4) * 128 + 128] = xin[m, :, i, :].astype(BF16)
            seg = xin[m, :, 16, :]
            of_query = jnp.sum(jnp.where(row == query, seg, 0.0), axis=0, keepdims=True)
            allowed = (query >= row) & (seg == of_query)
            mask[m] = jnp.where(allowed, 1.0, 0.0).astype(BF16)
            return carry

        lax.fori_loop(0, MICRO, load, 0)

    @pl.when(jnp.logical_not(first))
    def _():
        arrived(mask, mask_recv)

    next_z = jnp.where(half == 0, jnp.where(z == 0, 2, 1), jnp.where(z == 2, 0, 3))
    next_zhi = jnp.where(half == 0, zhi, 1 - zhi)
    next_x = jnp.where((half == 1) & (zhi == 1), x + 1, x)
    next_section, next_fsdp = next_x * 4 + next_zhi * 2 + core, y * 4 + next_z
    mask_copy = remote(mask, mask, mask_send, mask_recv, next_section, next_fsdp)

    @pl.when(jnp.logical_not(last))
    def _():
        mask_copy.start()

    def hop(m, j):
        return remote(
            xsend.at[m, j], xrecv.at[m, j], x_send.at[m * CHUNKS + j],
            x_recv.at[m * CHUNKS + j], next_section, next_fsdp,
        )

    owner_fsdp = y * 4 + jnp.where(z == 2, 0, 2) + core

    def delivery(m, s):
        return remote(
            staged.at[m, pl.ds(2 * s, 2)], owned.at[m], o_send.at[m * 16 + s], o_recv,
            s, owner_fsdp,
        )

    def one(m, carry):
        acc = jnp.zeros((SEQ, QKV), F32)
        squares = jnp.zeros((SEQ, 1), F32)
        for j in range(CHUNKS):
            @pl.when(jnp.logical_not(first))
            def _(j=j):
                arrived(xrecv.at[m, j], x_recv.at[m * CHUNKS + j])

            h = xrecv[m, j]
            hf = h.astype(F32)
            squares = squares + jnp.sum(hf * hf, axis=1, keepdims=True)
            acc = acc + jnp.dot(
                h, w1[2 * j : 2 * j + 2].reshape(CHUNK, QKV), preferred_element_type=F32
            )
        attended = attention(
            acc, squares, cos_ref[...], sin_ref[...], mask[m].astype(F32) > 0.5
        )
        for j in range(CHUNKS):
            update = jnp.dot(
                attended, w2[:, :, :, j * CHUNK : (j + 1) * CHUNK].reshape(QW, CHUNK),
                preferred_element_type=F32,
            )
            h = xrecv[m, j].astype(F32) + update

            @pl.when(jnp.logical_not(last))
            def _(j=j, h=h):
                xsend[m, j] = h.astype(BF16)
                hop(m, j).start()

            @pl.when(last)
            def _(j=j, h=h):
                for i in range(4):
                    staged[m, :, 4 * j + i, :] = h[:, 128 * i : 128 * i + 128]

        @pl.when(last)
        def _():
            def give(s, carry):
                delivery(m, s).start()
                return carry

            lax.fori_loop(0, 16, give, 0)

        return carry

    lax.fori_loop(0, MICRO, one, 0)

    arrived(owned, o_recv)
    out_ref[...] = owned[...]

    @pl.when(jnp.logical_not(in_self))
    def _():
        in_remote.wait_send()

    for is_self, far in z_copies:
        @pl.when(jnp.logical_not(is_self))
        def _(far=far):
            far.wait_send()

    for copy in sends:
        copy.wait_send()

    @pl.when(jnp.logical_not(last))
    def _():
        mask_copy.wait_send()

        def drain(n, carry):
            hop(n // CHUNKS, n % CHUNKS).wait_send()
            return carry

        lax.fori_loop(0, MICRO * CHUNKS, drain, 0)

    @pl.when(last)
    def _():
        def drain(n, carry):
            delivery(n // 16, n % 16).wait_send()
            return carry

        lax.fori_loop(0, MICRO * 16, drain, 0)


def shards(inputs, segments, norm_gains, w_query, w_keyval, w_output):
    rows = inputs[:, 0].astype(F32).reshape(MICRO, 2, 16, 128)
    segs = jnp.broadcast_to(segments[:, 0].astype(F32)[:, :, None, None], (MICRO, 2, 8, 128))
    positions = jnp.concatenate([rows, segs], axis=2)
    gains = norm_gains[0].astype(F32)[:, None]
    wa = jnp.concatenate([w_query[0], w_keyval[0]], axis=1).astype(F32) * gains
    cosine, sine = rope_tables()
    vmem = pl.BlockSpec(memory_space=pltpu.VMEM)
    hbm = pl.BlockSpec(memory_space=pl.ANY)
    dma = pltpu.SemaphoreType.DMA
    out = pl.pallas_call(
        kernel,
        out_shape=jax.ShapeDtypeStruct((MICRO, 2, 16, 128), F32),
        in_specs=[hbm, hbm, hbm, vmem, vmem],
        out_specs=vmem,
        scratch_shapes=[
            pltpu.VMEM((8, 2, 128, QKV), BF16),
            pltpu.VMEM((8, 2, 64, WIDTH), BF16),
            pltpu.VMEM((MICRO, SEQ, 24, 128), F32),
            pltpu.VMEM((MICRO, SEQ, 128), BF16),
            pltpu.VMEM((MICRO, CHUNKS, SEQ, CHUNK), BF16),
            pltpu.VMEM((MICRO, CHUNKS, SEQ, CHUNK), BF16),
            pltpu.VMEM((MICRO, SEQ, 16, 128), F32),
            pltpu.VMEM((MICRO, 2, 16, 128), F32),
            dma((4,)), dma((4,)), dma((16,)), dma((16,)), dma((18,)), dma((2,)),
            dma, dma, dma, dma, dma((16,)), dma((16,)), dma((64,)), dma,
        ],
        compiler_params=pltpu.CompilerParams(
            has_side_effects=True, vmem_limit_bytes=40 * 1024 * 1024
        ),
        name="stack",
    )(positions, wa.astype(BF16), w_output[0], jnp.asarray(cosine), jnp.asarray(sine))
    return out.astype(BF16).reshape(MICRO, 1, 2, WIDTH)


def solution(mesh):
    return jax.shard_map(
        shards,
        mesh=mesh,
        in_specs=(
            P(None, "fsdp", "section", None),
            P(None, "fsdp", "section"),
            P("section", "fsdp"),
            P("section", "fsdp", None),
            P("section", "fsdp", None),
            P("section", "fsdp", None),
        ),
        out_specs=P(None, "fsdp", "section", None),
        check_vma=False,
    )
```

```python
import jax
import jax.numpy as jnp
import numpy as np
from jax import lax
from jax.experimental import pallas as pl
from jax.experimental.pallas import tpu as pltpu
from jax.sharding import PartitionSpec as P

MESH = pl.DeviceIdType.MESH
BF16 = jnp.bfloat16
F32 = jnp.float32
EPSILON = 1e-05
THETA = 500000.0
SEQ = 32
MICRO = 4
WIDTH = 2048
CHUNKS = 4
CHUNK = WIDTH // CHUNKS
QW = 1024
KW = 256
QKV = 1536
LAST = 15


def rope_tables():
    position = np.arange(SEQ, dtype=np.float32)
    freq = (THETA ** (-np.arange(32, dtype=np.float32) * 2.0 / 64)).astype(np.float32)
    angle = (position[:, None] * freq[None, :]).astype(np.float32)
    c, s = np.cos(angle), np.sin(angle)
    return (
        np.concatenate([c, c, c, c], 1).astype(np.float32),
        np.concatenate([-s, s, -s, s], 1).astype(np.float32),
    )


def attention(accs, squares, cosine, sine, mask):
    scale = lax.rsqrt(squares * (1.0 / WIDTH) + EPSILON)
    cosine, sine = cosine * scale, sine * scale
    lane = lax.broadcasted_iota(jnp.int32, (SEQ, 128), 1)
    low, left = (lane & 63) < 32, lane < 64

    def rope(tile):
        swapped = jnp.where(low, pltpu.roll(tile, 96, 1), pltpu.roll(tile, 32, 1))
        return tile * cosine + swapped * sine

    zero = jnp.zeros((SEQ, 128), F32)
    block = lax.broadcasted_iota(jnp.int32, (64, 128), 1) // SEQ
    keys, values = [], []
    for i in range(2):
        key = rope(accs[4][:, 128 * i : 128 * i + 128])
        keys.append(jnp.transpose(jnp.concatenate([key] * 4, axis=0)))
        value = accs[5][:, 128 * i : 128 * i + 128] * scale
        other = pltpu.roll(value, 64, 1)
        for a, b in ((value, other), (other, value)):
            halves = [jnp.where(left, a, zero), jnp.where(left, zero, b)]
            values.append(jnp.concatenate(halves * 2, axis=0).astype(BF16))
    exps = []
    for g in range(4):
        key = keys[g // 2][64 * (g % 2) : 64 * (g % 2) + 64]
        spread = jnp.concatenate([jnp.where(block == h, key, 0.0) for h in range(4)], axis=0)
        query = jnp.concatenate(
            [rope(accs[g][:, 128 * i : 128 * i + 128]) for i in range(2)], axis=1
        )
        scores = jnp.dot(query.astype(BF16), spread.astype(BF16), preferred_element_type=F32)
        exps.append(jnp.where(mask, jnp.exp(scores * 0.125), 0.0))
    exps = jnp.concatenate(exps, axis=0)
    most = (exps * 0.99609375).astype(BF16)
    rest = (exps - most.astype(F32)).astype(BF16)
    row = lax.broadcasted_iota(jnp.int32, (128, 128), 0) // SEQ
    col = lax.broadcasted_iota(jnp.int32, (128, 128), 1) // SEQ
    same = jnp.where(row == col, 1.0, 0.0).astype(BF16)
    total = jnp.dot(most, same, preferred_element_type=F32) + jnp.dot(
        rest, same, preferred_element_type=F32
    )
    power = jnp.where(total > 1.0, 2.0**-8, 2.0**8)
    probs = (exps * power) * (1.0 / (total * power))
    outs = []
    for g in range(4):
        part = probs[SEQ * g : SEQ * g + SEQ]
        part = jnp.concatenate([jnp.where(left, part, 0.0), jnp.where(left, 0.0, part)], axis=0)
        mixed = jnp.dot(part.astype(BF16), values[g], preferred_element_type=F32).astype(BF16)
        outs += [mixed[:SEQ], mixed[SEQ:]]
    return jnp.concatenate(outs, axis=1)


def kernel(
    in_ref, seg_ref, wa_ref, wb_ref, cos_ref, sin_ref, out_ref,
    w1, w2, xin, segs, wide, mask, xrecv, xsend, staged, owned,
    z_send, z_recv, ring_send, ring_recv, sib_send, sib_recv, cross_send, cross_recv,
    in_send, in_recv, mask_send, mask_recv, x_send, x_recv, o_send, o_recv,
):
    section, fsdp = lax.axis_index("section"), lax.axis_index("fsdp")
    x, zhi, core = section // 4, (section // 2) % 2, section % 2
    y, zlo = fsdp // 4, fsdp % 4
    z = zhi * 4 + zlo
    side = ((x + 1) // 2) % 2
    layer = jnp.where(x < 2, (z + 6) % 8, 8 + (9 - z) % 8)
    first, last = layer == 0, layer == LAST
    plane = section - core

    def place(at_x, at_z, at_core):
        return at_x * 4 + (at_z // 4) * 2 + at_core, y * 4 + at_z % 4

    def host(of_layer, of_side, at_core):
        early = of_layer < 8
        at_x = jnp.where(early, of_side, 3 - of_side)
        return place(at_x, jnp.where(early, of_layer + 2, 17 - of_layer) % 8, at_core)

    def remote(src, dst, send, recv, to):
        return pltpu.make_async_remote_copy(
            src_ref=src, dst_ref=dst, send_sem=send, recv_sem=recv,
            device_id=to, device_id_type=MESH,
        )

    def is_me(to):
        return (to[0] == section) & (to[1] == fsdp)

    sibling = (plane + 1 - core, fsdp)
    partner = place(jnp.where(x < 2, 1 - x, 5 - x), z, core)
    right = (section, ((y + 1) % 8) * 4 + zlo)
    left = (section, ((y + 7) % 8) * 4 + zlo)

    def arrived(dst, recv):
        remote(dst, dst, z_send.at[0], recv, sibling).wait_recv()

    in_to = host(jnp.int32(0), zlo // 2, zlo % 2)
    own_layer = section
    a_to = host(own_layer, zlo // 2, zlo % 2)
    b_to = [host(own_layer, q, zlo // 2) for q in range(2)]
    next_to = host(jnp.minimum(layer + 1, LAST), side, core)
    prev_from = host(jnp.maximum(layer - 1, 0), side, core)
    owner_fsdp = y * 4 + 2 * side + core
    result_from = host(jnp.int32(LAST), zlo // 2, zlo % 2)
    a_from = (layer, y * 4 + 2 * side + core)
    b_from = [(layer, y * 4 + 2 * core + u) for u in range(2)]

    barrier = pltpu.get_barrier_semaphore()

    def hello(to):
        pl.semaphore_signal(barrier, inc=1, device_id=to, device_id_type=MESH)

    def hello_other(to):
        @pl.when(jnp.logical_not(is_me(to)))
        def _():
            hello(to)

    for to in (right, left, sibling, partner):
        hello(to)
    for to in [a_from] + b_from + [result_from]:
        hello_other(to)

    @pl.when(jnp.logical_not(first))
    def _():
        hello(prev_from)

    def hello_all(s, carry):
        hello_other((s, owner_fsdp))
        return carry

    @pl.when(first)
    def _():
        lax.fori_loop(0, 16, hello_all, 0)

    def other(to):
        return jnp.where(is_me(to), 0, 1)

    own_share = jnp.where(owner_fsdp == fsdp, 15, 16)
    expected = 4 + other(in_to) + other(a_to) + other(b_to[0]) + other(b_to[1])
    pl.semaphore_wait(barrier, expected + jnp.where(last, own_share, 1))

    started = []

    def give(src, dst, send, recv, to):
        far = remote(src, dst, send, recv, to)
        near = pltpu.make_async_copy(src, dst, recv)

        @pl.when(is_me(to))
        def _():
            near.start()

        @pl.when(jnp.logical_not(is_me(to)))
        def _():
            far.start()

        started.append((is_me(to), far))

    give(wa_ref, w1.at[y, zlo // 2, zlo % 2], z_send.at[0], z_recv.at[0], a_to)
    for q in range(2):
        give(wb_ref, w2.at[y, zlo // 2, zlo % 2], z_send.at[1 + q], z_recv.at[1 + zlo % 2], b_to[q])
    give(in_ref, xin.at[:, pl.ds(2 * section, 2)], in_send.at[0], in_recv.at[0], in_to)
    give(seg_ref, segs.at[section], in_send.at[1], in_recv.at[1], in_to)

    sends = []

    def send(ref, sems, recv, to):
        copy = remote(ref, ref, sems.at[len([1 for kind, _ in sends if kind is sems])], recv, to)
        copy.start()
        sends.append((sems, copy))

    def ring(ref, direction, step, part):
        recv = ring_recv.at[(direction * 4 + step) * 3 + part]
        send(ref, ring_send, recv, right if direction == 0 else left)

    def cross(ref, column):
        send(ref, cross_send, cross_recv.at[column], partner)

    def across(ref, part):
        send(ref, sib_send, sib_recv.at[part], sibling)

    def column_of(direction, step):
        return (y + (8 - step if direction == 0 else step)) % 8

    def ring_last(column, direction):
        ref = w1.at[column, side, core]
        return remote(
            ref, ref, ring_send.at[15], ring_recv.at[(direction * 4 + 3) * 3],
            right if direction == 0 else left,
        )

    def w1_at(column):
        return w1.at[column, side, core]

    def w2_at(column, u):
        return w2.at[column, core, u]

    def w2_both(column):
        return w2.at[column, core]

    arrived(w1_at(y), z_recv.at[0])
    for direction in range(2):
        ring(w1_at(y), direction, 0, 0)
    cross(w1_at(y), y)
    across(w1_at(y), 0)
    for u in range(2):
        arrived(w2_at(y, u), z_recv.at[1 + u])
    for direction in range(2):
        ring(w2_both(y), direction, 0, 1)
    across(w2_both(y), 1)

    def crossed(column):
        ref = w1.at[column, 1 - side, core]
        arrived(ref, cross_recv.at[column])
        across(ref, 0)

    for step in range(1, 4):
        for direction in range(2):
            column = column_of(direction, step)
            arrived(w1_at(column), ring_recv.at[(direction * 4 + step - 1) * 3])
            if step < 3:
                ring(w1_at(column), direction, step, 0)
            else:
                @pl.when(core == direction)
                def _(column=column, direction=direction):
                    ring_last(column, direction).start()
            cross(w1_at(column), column)
            across(w1_at(column), 0)
        for direction in range(2):
            column = column_of(direction, step)
            arrived(w2_both(column), ring_recv.at[(direction * 4 + step - 1) * 3 + 1])
            ring(w2_both(column) if step < 3 else w2_at(column, direction), direction, step, 1)
            across(w2_both(column), 1)
        if step == 1:
            crossed(y)
        else:
            for direction in range(2):
                crossed(column_of(direction, step - 1))
    column = (y + 4) % 8
    for direction in range(2):
        @pl.when(core == direction)
        def _(direction=direction):
            arrived(w1_at(column), ring_recv.at[(direction * 4 + 3) * 3])
    cross(w1_at(column), column)
    across(w1_at(column), 0)
    for direction in range(2):
        arrived(w2_at(column, direction), ring_recv.at[(direction * 4 + 3) * 3 + 1])
        across(w2_at(column, direction), 1)
    for direction in range(2):
        crossed(column_of(direction, 3))
    crossed(column)
    arrived(w1.at[:, :, 1 - core], sib_recv.at[0])
    arrived(w2.at[:, 1 - core], sib_recv.at[1])

    def local(m, j):
        return pltpu.make_async_copy(xsend.at[m, j], xrecv.at[m, j], x_recv.at[m * CHUNKS + j])

    @pl.when(first)
    def _():
        arrived(xin, in_recv.at[0])
        arrived(segs, in_recv.at[1])
        row = lax.broadcasted_iota(jnp.int32, (SEQ, 128), 0)
        key = lax.broadcasted_iota(jnp.int32, (SEQ, 128), 1) % SEQ
        to = lax.broadcasted_iota(jnp.int32, (SEQ, SEQ), 0)
        source = lax.broadcasted_iota(jnp.int32, (SEQ, SEQ), 1)
        order = jnp.where(to == 2 * (source % 16) + source // 16, 1.0, 0.0).astype(BF16)

        def load(m, carry):
            wide[...] = xin[m].astype(F32)
            for i in range(16):
                xsend[m, i // 4, :, (i % 4) * 128 : (i % 4) * 128 + 128] = wide[:, i, :].astype(BF16)
            for j in range(CHUNKS):
                local(m, j).start()
            return carry

        lax.fori_loop(0, MICRO, load, 0)
        for m in range(MICRO):
            seg = jnp.concatenate([segs[:, 2 * m, :], segs[:, 2 * m + 1, :]], axis=0)
            seg = jnp.dot(order, seg.astype(BF16), preferred_element_type=F32)
            of_key = jnp.sum(jnp.where(row == key, seg, 0.0), axis=0, keepdims=True)
            allowed = (row >= key) & (seg == of_key)
            mask[m] = jnp.where(allowed, 1.0, 0.0).astype(BF16)

    @pl.when(jnp.logical_not(first))
    def _():
        arrived(mask, mask_recv)

    mask_copy = remote(mask, mask, mask_send, mask_recv, next_to)

    @pl.when(jnp.logical_not(last))
    def _():
        mask_copy.start()

    def hop(m, j):
        n = m * CHUNKS + j
        return remote(xsend.at[m, j], xrecv.at[m, j], x_send.at[n], x_recv.at[n], next_to)

    def delivery(m, s):
        return remote(
            staged.at[m, pl.ds(2 * s, 2)], owned.at[m], o_send.at[m * 16 + s], o_recv,
            (s, owner_fsdp),
        )

    def keep(m):
        return pltpu.make_async_copy(staged.at[m, pl.ds(2 * section, 2)], owned.at[m], o_recv)

    def one(m, carry):
        accs = [None] * 6
        squares = jnp.zeros((SEQ, 1), F32)
        for j in range(CHUNKS):
            arrived(xrecv.at[m, j], x_recv.at[m * CHUNKS + j])
            h = xrecv[m, j]
            hf = h.astype(F32)
            squares = squares + jnp.sum(hf * hf, axis=1, keepdims=True)
            for n in (4, 5, 0, 1, 2, 3):
                weight = w1[2 * j : 2 * j + 2, :, :, :, 256 * n : 256 * n + 256]
                term = jnp.dot(h, weight.reshape(CHUNK, 256), preferred_element_type=F32)
                accs[n] = term if accs[n] is None else accs[n] + term
        attended = attention(accs, squares, cos_ref[...], sin_ref[...], mask[m].astype(F32) > 0.5)
        for j in range(CHUNKS):
            weight = w2[:, :, :, :, j * CHUNK : (j + 1) * CHUNK].reshape(QW, CHUNK)
            update = jnp.dot(attended, weight, preferred_element_type=F32)
            h = xrecv[m, j].astype(F32) + update

            @pl.when(jnp.logical_not(last))
            def _(j=j, h=h):
                xsend[m, j] = h.astype(BF16)
                hop(m, j).start()

            @pl.when(last)
            def _(j=j, h=h):
                for i in range(4):
                    wide[:, 4 * j + i, :] = h[:, 128 * i : 128 * i + 128]

        @pl.when(last)
        def _():
            staged[m] = wide[...].astype(BF16)

            def hand(s, carry):
                mine = (s == section) & (owner_fsdp == fsdp)

                @pl.when(mine)
                def _():
                    keep(m).start()

                @pl.when(jnp.logical_not(mine))
                def _():
                    delivery(m, s).start()

                return carry

            lax.fori_loop(0, 16, hand, 0)

        return carry

    lax.fori_loop(0, MICRO, one, 0)

    arrived(owned, o_recv)
    out_ref[...] = owned[...]

    for mine, far in started:
        @pl.when(jnp.logical_not(mine))
        def _(far=far):
            far.wait_send()

    for _, copy in sends:
        copy.wait_send()
    for direction in range(2):
        @pl.when(core == direction)
        def _(direction=direction):
            ring_last(column_of(direction, 3), direction).wait_send()

    @pl.when(jnp.logical_not(last))
    def _():
        mask_copy.wait_send()

        def drain(n, carry):
            hop(n // CHUNKS, n % CHUNKS).wait_send()
            return carry

        lax.fori_loop(0, MICRO * CHUNKS, drain, 0)

    @pl.when(last)
    def _():
        def drain(n, carry):
            @pl.when(jnp.logical_not((n % 16 == section) & (owner_fsdp == fsdp)))
            def _():
                delivery(n // 16, n % 16).wait_send()

            return carry

        lax.fori_loop(0, MICRO * 16, drain, 0)


def shards(inputs, segments, norm_gains, w_query, w_keyval, w_output):
    positions = inputs[:, 0].reshape(MICRO, 2, 16, 128)
    segs = jnp.broadcast_to(segments[:, 0].reshape(MICRO * 2, 1), (MICRO * 2, 128)).astype(F32)
    gains = norm_gains[0].astype(F32)[:, None]
    wa = jnp.concatenate([w_query[0], w_keyval[0]], axis=1).astype(F32) * gains
    cosine, sine = rope_tables()
    vmem = pl.BlockSpec(memory_space=pltpu.VMEM)
    hbm = pl.BlockSpec(memory_space=pl.ANY)
    dma = pltpu.SemaphoreType.DMA
    out = pl.pallas_call(
        kernel,
        out_shape=jax.ShapeDtypeStruct((MICRO, 2, 16, 128), BF16),
        in_specs=[hbm, hbm, hbm, hbm, vmem, vmem],
        out_specs=vmem,
        scratch_shapes=[
            pltpu.VMEM((8, 2, 2, 64, QKV), BF16),
            pltpu.VMEM((8, 2, 2, 32, WIDTH), BF16),
            pltpu.VMEM((MICRO, SEQ, 16, 128), BF16),
            pltpu.VMEM((16, MICRO * 2, 128), F32),
            pltpu.VMEM((SEQ, 16, 128), F32),
            pltpu.VMEM((MICRO, SEQ, 128), BF16),
            pltpu.VMEM((MICRO, CHUNKS, SEQ, CHUNK), BF16),
            pltpu.VMEM((MICRO, CHUNKS, SEQ, CHUNK), BF16),
            pltpu.VMEM((MICRO, SEQ, 16, 128), BF16),
            pltpu.VMEM((MICRO, 2, 16, 128), BF16),
            dma((3,)), dma((3,)), dma((16,)), dma((24,)), dma((32,)), dma((2,)), dma((8,)), dma((8,)),
            dma((2,)), dma((2,)), dma, dma, dma((16,)), dma((16,)), dma((64,)), dma,
        ],
        compiler_params=pltpu.CompilerParams(
            collective_id=0, has_side_effects=True, vmem_limit_bytes=40 * 1024 * 1024
        ),
        name="stack",
    )(positions, segs, wa.astype(BF16), w_output[0], jnp.asarray(cosine), jnp.asarray(sine))
    return out.reshape(MICRO, 1, 2, WIDTH)


def solution(mesh):
    return jax.shard_map(
        shards,
        mesh=mesh,
        in_specs=(
            P(None, "fsdp", "section", None),
            P(None, "fsdp", "section"),
            P("section", "fsdp"),
            P("section", "fsdp", None),
            P("section", "fsdp", None),
            P("section", "fsdp", None),
        ),
        out_specs=P(None, "fsdp", "section", None),
        check_vma=False,
    )
```

```python
import jax
import jax.numpy as jnp
import numpy as np
from jax import lax
from jax.experimental import pallas as pl
from jax.experimental.pallas import tpu as pltpu
from jax.sharding import PartitionSpec as P

MESH = pl.DeviceIdType.MESH
BF16 = jnp.bfloat16
F32 = jnp.float32
EPSILON = 1e-05
THETA = 500000.0
SEQ = 32
MICRO = 4
WIDTH = 2048
CHUNKS = 4
CHUNK = WIDTH // CHUNKS
TILES = CHUNK // 128
QW = 1024
KW = 256
QKV = 1536
LAST = 15


def rope_tables():
    position = np.arange(SEQ, dtype=np.float32)
    freq = (THETA ** (-np.arange(32, dtype=np.float32) * 2.0 / 64)).astype(np.float32)
    angle = (position[:, None] * freq[None, :]).astype(np.float32)
    c, s = np.cos(angle), np.sin(angle)
    return (
        np.concatenate([c, c, c, c], 1).astype(np.float32),
        np.concatenate([-s, s, -s, s], 1).astype(np.float32),
    )


def attention(accs, squares, cosine, sine, mask):
    scale = lax.rsqrt(squares * (1.0 / WIDTH) + EPSILON)
    cosine, sine = cosine * scale, sine * scale
    lane = lax.broadcasted_iota(jnp.int32, (SEQ, 128), 1)
    low, left = (lane & 63) < 32, lane < 64

    def rope(tile):
        swapped = jnp.where(low, pltpu.roll(tile, 96, 1), pltpu.roll(tile, 32, 1))
        return tile * cosine + swapped * sine

    zero = jnp.zeros((SEQ, 128), F32)
    block = lax.broadcasted_iota(jnp.int32, (64, 128), 1) // SEQ
    keys, values = [], []
    for i in range(2):
        key = rope(accs[4][:, 128 * i : 128 * i + 128])
        keys.append(jnp.transpose(jnp.concatenate([key] * 4, axis=0)))
        value = accs[5][:, 128 * i : 128 * i + 128] * scale
        other = pltpu.roll(value, 64, 1)
        for a, b in ((value, other), (other, value)):
            halves = [jnp.where(left, a, zero), jnp.where(left, zero, b)]
            values.append(jnp.concatenate(halves * 2, axis=0).astype(BF16))
    exps = []
    for g in range(4):
        key = keys[g // 2][64 * (g % 2) : 64 * (g % 2) + 64]
        spread = jnp.concatenate([jnp.where(block == h, key, 0.0) for h in range(4)], axis=0)
        query = jnp.concatenate(
            [rope(accs[g][:, 128 * i : 128 * i + 128]) for i in range(2)], axis=1
        )
        scores = jnp.dot(query.astype(BF16), spread.astype(BF16), preferred_element_type=F32)
        exps.append(jnp.where(mask, jnp.exp(scores * 0.125), 0.0))
    exps = jnp.concatenate(exps, axis=0)
    most = (exps * 0.99609375).astype(BF16)
    rest = (exps - most.astype(F32)).astype(BF16)
    row = lax.broadcasted_iota(jnp.int32, (256, 128), 0) % 128 // SEQ
    col = lax.broadcasted_iota(jnp.int32, (256, 128), 1) // SEQ
    same = jnp.where(row == col, 1.0, 0.0).astype(BF16)
    total = jnp.dot(jnp.concatenate([most, rest], axis=1), same, preferred_element_type=F32)
    power = jnp.where(total > 1.0, 2.0**-8, 2.0**8)
    probs = (exps * power) * (1.0 / (total * power))
    outs = []
    for g in range(4):
        part = probs[SEQ * g : SEQ * g + SEQ]
        part = jnp.concatenate([jnp.where(left, part, 0.0), jnp.where(left, 0.0, part)], axis=0)
        mixed = jnp.dot(part.astype(BF16), values[g], preferred_element_type=F32).astype(BF16)
        outs += [mixed[:SEQ], mixed[SEQ:]]
    return jnp.concatenate(outs, axis=1)


def kernel(
    in_ref, seg_ref, wa_ref, wb_ref, cos_ref, sin_ref, out_ref,
    w1, w2, xin, segs, wide, mask, xrecv, xsend, staged, owned,
    z_send, z_recv, ring_send, ring_recv, sib_send, sib_recv, cross_send, cross_recv,
    in_send, in_recv, mask_send, mask_recv, x_send, x_recv, o_send, o_recv,
):
    section, fsdp = lax.axis_index("section"), lax.axis_index("fsdp")
    x, zhi, core = section // 4, (section // 2) % 2, section % 2
    y, zlo = fsdp // 4, fsdp % 4
    z = zhi * 4 + zlo
    side = ((x + 1) // 2) % 2
    layer = jnp.where(x < 2, (z + 7) % 8, 8 + (8 - z) % 8)
    first, last = layer == 0, layer == LAST
    plane = section - core

    def place(at_x, at_z, at_core):
        return at_x * 4 + (at_z // 4) * 2 + at_core, y * 4 + at_z % 4

    def host(of_layer, of_side, at_core):
        early = of_layer < 8
        at_x = jnp.where(early, of_side, 3 - of_side)
        return place(at_x, jnp.where(early, of_layer + 1, 16 - of_layer) % 8, at_core)

    def remote(src, dst, send, recv, to):
        return pltpu.make_async_remote_copy(
            src_ref=src, dst_ref=dst, send_sem=send, recv_sem=recv,
            device_id=to, device_id_type=MESH,
        )

    def is_me(to):
        return (to[0] == section) & (to[1] == fsdp)

    sibling = (plane + 1 - core, fsdp)
    partner = place(jnp.where(x < 2, 1 - x, 5 - x), z, core)
    right = (section, ((y + 1) % 8) * 4 + zlo)
    left = (section, ((y + 7) % 8) * 4 + zlo)

    def arrived(dst, recv):
        remote(dst, dst, z_send.at[0], recv, sibling).wait_recv()

    in_to = host(jnp.int32(0), zlo // 2, zlo % 2)
    own_layer = section
    a_to = host(own_layer, zlo // 2, zlo % 2)
    b_to = [host(own_layer, q, zlo // 2) for q in range(2)]
    next_to = host(jnp.minimum(layer + 1, LAST), side, core)
    prev_from = host(jnp.maximum(layer - 1, 0), side, core)
    owner_fsdp = y * 4 + 2 * side + core
    result_from = host(jnp.int32(LAST), zlo // 2, zlo % 2)
    a_from = (layer, y * 4 + 2 * side + core)
    b_from = [(layer, y * 4 + 2 * core + u) for u in range(2)]

    barrier = pltpu.get_barrier_semaphore()

    def hello(to):
        pl.semaphore_signal(barrier, inc=1, device_id=to, device_id_type=MESH)

    def hello_other(to):
        @pl.when(jnp.logical_not(is_me(to)))
        def _():
            hello(to)

    for to in (right, left, sibling, partner):
        hello(to)

    for to in [a_from] + b_from + [result_from]:
        hello_other(to)

    @pl.when(jnp.logical_not(first))
    def _():
        hello(prev_from)

    def hello_all(s, carry):
        hello_other((s, owner_fsdp))
        return carry

    @pl.when(first)
    def _():
        lax.fori_loop(0, 16, hello_all, 0)

    def other(to):
        return jnp.where(is_me(to), 0, 1)

    own_share = jnp.where(owner_fsdp == fsdp, 15, 16)
    expected = 4 + other(in_to) + other(a_to) + other(b_to[0]) + other(b_to[1])
    pl.semaphore_wait(barrier, expected + jnp.where(last, own_share, 1))

    def give(src, dst, send, recv, to):
        @pl.when(is_me(to))
        def _():
            pltpu.make_async_copy(src, dst, recv).start()

        @pl.when(jnp.logical_not(is_me(to)))
        def _():
            remote(src, dst, send, recv, to).start()

    def given(src, dst, send, recv, to):
        @pl.when(jnp.logical_not(is_me(to)))
        def _():
            remote(src, dst, send, recv, to).wait_send()

    own_a = (wa_ref, w1.at[y, zlo // 2, zlo % 2], z_send.at[0], z_recv.at[0], a_to)
    own_b = [
        (wb_ref, w2.at[y, zlo // 2, zlo % 2], z_send.at[1 + q], z_recv.at[1 + zlo % 2], b_to[q])
        for q in range(2)
    ]
    own_in = [
        (in_ref, xin.at[:, pl.ds(2 * section, 2)], in_send.at[0], in_recv.at[0], in_to),
        (seg_ref, segs.at[section], in_send.at[1], in_recv.at[1], in_to),
    ]

    give(*own_a)
    given(*own_a)
    for copy in own_in + own_b:
        give(*copy)

    sends = []

    def send(ref, sems, recv, to):
        copy = remote(ref, ref, sems.at[len([1 for kind, _ in sends if kind is sems])], recv, to)
        copy.start()
        sends.append((sems, copy))

    def ring(ref, direction, step, part):
        recv = ring_recv.at[(direction * 4 + step) * 3 + part]
        send(ref, ring_send, recv, right if direction == 0 else left)

    def cross(ref, column):
        send(ref, cross_send, cross_recv.at[column], partner)

    def across(ref, part):
        send(ref, sib_send, sib_recv.at[part], sibling)

    def column_of(direction, step):
        return (y + (8 - step if direction == 0 else step)) % 8

    def ring_last(column, direction):
        ref = w1.at[column, side, core]
        return remote(
            ref, ref, ring_send.at[15], ring_recv.at[(direction * 4 + 3) * 3],
            right if direction == 0 else left,
        )

    def w1_at(column):
        return w1.at[column, side, core]

    def w2_at(column, u):
        return w2.at[column, core, u]

    def w2_both(column):
        return w2.at[column, core]

    arrived(w1_at(y), z_recv.at[0])
    for direction in range(2):
        ring(w1_at(y), direction, 0, 0)
    cross(w1_at(y), y)
    across(w1_at(y), 0)
    for u in range(2):
        arrived(w2_at(y, u), z_recv.at[1 + u])
    for direction in range(2):
        ring(w2_both(y), direction, 0, 1)
    across(w2_both(y), 1)

    def crossed(column):
        ref = w1.at[column, 1 - side, core]
        arrived(ref, cross_recv.at[column])
        across(ref, 0)

    for step in range(1, 4):
        for direction in range(2):
            column = column_of(direction, step)
            arrived(w1_at(column), ring_recv.at[(direction * 4 + step - 1) * 3])
            if step < 3:
                ring(w1_at(column), direction, step, 0)
            else:
                @pl.when(core == direction)
                def _(column=column, direction=direction):
                    ring_last(column, direction).start()
            cross(w1_at(column), column)
            across(w1_at(column), 0)
        for direction in range(2):
            column = column_of(direction, step)
            arrived(w2_both(column), ring_recv.at[(direction * 4 + step - 1) * 3 + 1])
            ring(w2_both(column) if step < 3 else w2_at(column, direction), direction, step, 1)
            across(w2_both(column), 1)
        if step == 1:
            crossed(y)
        else:
            for direction in range(2):
                crossed(column_of(direction, step - 1))
    def local(m, j):
        return pltpu.make_async_copy(xsend.at[m, j], xrecv.at[m, j], x_recv.at[m * CHUNKS + j])

    @pl.when(first)
    def _():
        arrived(xin, in_recv.at[0])
        arrived(segs, in_recv.at[1])
        row = lax.broadcasted_iota(jnp.int32, (SEQ, 128), 0)
        key = lax.broadcasted_iota(jnp.int32, (SEQ, 128), 1) % SEQ
        to = lax.broadcasted_iota(jnp.int32, (SEQ, SEQ), 0)
        source = lax.broadcasted_iota(jnp.int32, (SEQ, SEQ), 1)
        order = jnp.where(to == 2 * (source % 16) + source // 16, 1.0, 0.0).astype(BF16)

        def load(m, carry):
            wide[...] = xin[m].astype(F32)
            for i in range(16):
                xsend[m, i // TILES, :, (i % TILES) * 128 : (i % TILES) * 128 + 128] = wide[:, i, :].astype(BF16)
            for j in range(CHUNKS):
                local(m, j).start()
            return carry

        lax.fori_loop(0, MICRO, load, 0)
        for m in range(MICRO):
            seg = jnp.concatenate([segs[:, 2 * m, :], segs[:, 2 * m + 1, :]], axis=0)
            seg = jnp.dot(order, seg.astype(BF16), preferred_element_type=F32)
            of_key = jnp.sum(jnp.where(row == key, seg, 0.0), axis=0, keepdims=True)
            allowed = (row >= key) & (seg == of_key)
            mask[m] = jnp.where(allowed, 1.0, 0.0).astype(BF16)

    column = (y + 4) % 8
    for direction in range(2):
        @pl.when(core == direction)
        def _(direction=direction):
            arrived(w1_at(column), ring_recv.at[(direction * 4 + 3) * 3])
    cross(w1_at(column), column)
    across(w1_at(column), 0)
    for direction in range(2):
        arrived(w2_at(column, direction), ring_recv.at[(direction * 4 + 3) * 3 + 1])
        across(w2_at(column, direction), 1)
    for direction in range(2):
        crossed(column_of(direction, 3))
    crossed(column)
    arrived(w1.at[:, :, 1 - core], sib_recv.at[0])
    arrived(w2.at[:, 1 - core], sib_recv.at[1])

    @pl.when(jnp.logical_not(first))
    def _():
        arrived(mask, mask_recv)

    mask_copy = remote(mask, mask, mask_send, mask_recv, next_to)

    @pl.when(jnp.logical_not(last))
    def _():
        mask_copy.start()

    def hop(m, j):
        n = m * CHUNKS + j
        return remote(xsend.at[m, j], xrecv.at[m, j], x_send.at[n], x_recv.at[n], next_to)

    def delivery(m, s):
        return remote(
            staged.at[m, pl.ds(2 * s, 2)], owned.at[m], o_send.at[m * 16 + s], o_recv,
            (s, owner_fsdp),
        )

    def keep(m):
        return pltpu.make_async_copy(staged.at[m, pl.ds(2 * section, 2)], owned.at[m], o_recv)

    def one(m, final):
        accs = [None] * 6
        squares = jnp.zeros((SEQ, 1), F32)
        span = 8 // CHUNKS
        for j in range(CHUNKS):
            arrived(xrecv.at[m, j], x_recv.at[m * CHUNKS + j])
            h = xrecv[m, j]
            hf = h.astype(F32)
            squares = squares + jnp.sum(hf * hf, axis=1, keepdims=True)
            for n in (4, 5, 0, 1, 2, 3):
                weight = w1[span * j : span * (j + 1), :, :, :, 256 * n : 256 * n + 256]
                term = jnp.dot(h, weight.reshape(CHUNK, 256), preferred_element_type=F32)
                accs[n] = term if accs[n] is None else accs[n] + term
        attended = attention(accs, squares, cos_ref[...], sin_ref[...], mask[m].astype(F32) > 0.5)
        for j in range(CHUNKS):
            weight = w2[:, :, :, :, j * CHUNK : (j + 1) * CHUNK].reshape(QW, CHUNK)
            update = jnp.dot(attended, weight, preferred_element_type=F32)
            h = xrecv[m, j].astype(F32) + update
            if final:
                for i in range(TILES):
                    wide[:, TILES * j + i, :] = h[:, 128 * i : 128 * i + 128]
            else:
                xsend[m, j] = h.astype(BF16)
                hop(m, j).start()

        if final:
            staged[m] = wide[...].astype(BF16)

            def hand(s, carry):
                mine = (s == section) & (owner_fsdp == fsdp)

                @pl.when(mine)
                def _():
                    keep(m).start()

                @pl.when(jnp.logical_not(mine))
                def _():
                    delivery(m, s).start()

                return carry

            lax.fori_loop(0, 16, hand, 0)

    def run(final):
        def step(m, carry):
            one(m, final)
            return carry

        lax.fori_loop(0, MICRO, step, 0)

    @pl.when(last)
    def _():
        run(True)

    @pl.when(jnp.logical_not(last))
    def _():
        run(False)

    arrived(owned, o_recv)
    out_ref[...] = owned[...]

    for copy in own_b + own_in:
        given(*copy)
    for _, copy in sends:
        copy.wait_send()
    for direction in range(2):
        @pl.when(core == direction)
        def _(direction=direction):
            ring_last(column_of(direction, 3), direction).wait_send()

    @pl.when(jnp.logical_not(last))
    def _():
        mask_copy.wait_send()

        def drain(n, carry):
            hop(n // CHUNKS, n % CHUNKS).wait_send()
            return carry

        lax.fori_loop(0, MICRO * CHUNKS, drain, 0)

    @pl.when(last)
    def _():
        def drain(n, carry):
            @pl.when(jnp.logical_not((n % 16 == section) & (owner_fsdp == fsdp)))
            def _():
                delivery(n // 16, n % 16).wait_send()

            return carry

        lax.fori_loop(0, MICRO * 16, drain, 0)


def shards(inputs, segments, norm_gains, w_query, w_keyval, w_output):
    positions = inputs[:, 0].reshape(MICRO, 2, 16, 128)
    segs = jnp.broadcast_to(segments[:, 0].reshape(MICRO * 2, 1), (MICRO * 2, 128)).astype(F32)
    gains = norm_gains[0].astype(F32)[:, None]
    wa = jnp.concatenate([w_query[0], w_keyval[0]], axis=1).astype(F32) * gains
    cosine, sine = rope_tables()
    vmem = pl.BlockSpec(memory_space=pltpu.VMEM)
    hbm = pl.BlockSpec(memory_space=pl.ANY)
    dma = pltpu.SemaphoreType.DMA
    hops = MICRO * CHUNKS
    out = pl.pallas_call(
        kernel,
        out_shape=jax.ShapeDtypeStruct((MICRO, 2, 16, 128), BF16),
        in_specs=[hbm, hbm, hbm, hbm, vmem, vmem],
        out_specs=vmem,
        scratch_shapes=[
            pltpu.VMEM((8, 2, 2, 64, QKV), BF16),
            pltpu.VMEM((8, 2, 2, 32, WIDTH), BF16),
            pltpu.VMEM((MICRO, SEQ, 16, 128), BF16),
            pltpu.VMEM((16, MICRO * 2, 128), F32),
            pltpu.VMEM((SEQ, 16, 128), F32),
            pltpu.VMEM((MICRO, SEQ, 128), BF16),
            pltpu.VMEM((MICRO, CHUNKS, SEQ, CHUNK), BF16),
            pltpu.VMEM((MICRO, CHUNKS, SEQ, CHUNK), BF16),
            pltpu.VMEM((MICRO, SEQ, 16, 128), BF16),
            pltpu.VMEM((MICRO, 2, 16, 128), BF16),
            dma((3,)), dma((3,)), dma((16,)), dma((24,)), dma((32,)), dma((2,)), dma((8,)), dma((8,)),
            dma((2,)), dma((2,)), dma, dma, dma((hops,)), dma((hops,)), dma((64,)), dma,
        ],
        compiler_params=pltpu.CompilerParams(
            collective_id=0, has_side_effects=True, vmem_limit_bytes=40 * 1024 * 1024
        ),
        name="stack",
    )(positions, segs, wa.astype(BF16), w_output[0], jnp.asarray(cosine), jnp.asarray(sine))
    return out.reshape(MICRO, 1, 2, WIDTH)


def solution(mesh):
    return jax.shard_map(
        shards,
        mesh=mesh,
        in_specs=(
            P(None, "fsdp", "section", None),
            P(None, "fsdp", "section"),
            P("section", "fsdp"),
            P("section", "fsdp", None),
            P("section", "fsdp", None),
            P("section", "fsdp", None),
        ),
        out_specs=P(None, "fsdp", "section", None),
        check_vma=False,
    )
```

```python
import jax
import jax.numpy as jnp
import numpy as np
from jax import lax
from jax.experimental import pallas as pl
from jax.experimental.pallas import tpu as pltpu
from jax.sharding import PartitionSpec as P

MESH = pl.DeviceIdType.MESH
BF16 = jnp.bfloat16
F32 = jnp.float32
EPSILON = 1e-05
THETA = 500000.0
SEQ = 32
MICRO = 4
WIDTH = 2048
CHUNKS = 4
CHUNK = WIDTH // CHUNKS
TILES = CHUNK // 128
QW = 1024
KW = 256
QKV = 1536
LAST = 15


def rope_tables():
    position = np.arange(SEQ, dtype=np.float32)
    freq = (THETA ** (-np.arange(32, dtype=np.float32) * 2.0 / 64)).astype(np.float32)
    angle = (position[:, None] * freq[None, :]).astype(np.float32)
    c, s = np.cos(angle), np.sin(angle)
    return (
        np.concatenate([c, c, c, c], 1).astype(np.float32),
        np.concatenate([-s, s, -s, s], 1).astype(np.float32),
    )


def attention(accs, squares, cosine, sine, mask):
    scale = lax.rsqrt(squares * (1.0 / WIDTH) + EPSILON)
    cosine, sine = cosine * scale, sine * scale
    lane = lax.broadcasted_iota(jnp.int32, (SEQ, 128), 1)
    low, left = (lane & 63) < 32, lane < 64

    def rope(tile):
        swapped = jnp.where(low, pltpu.roll(tile, 96, 1), pltpu.roll(tile, 32, 1))
        return tile * cosine + swapped * sine

    zero = jnp.zeros((SEQ, 128), F32)
    block = lax.broadcasted_iota(jnp.int32, (64, 128), 1) // SEQ
    keys, values = [], []
    for i in range(2):
        key = rope(accs[4][:, 128 * i : 128 * i + 128])
        keys.append(jnp.transpose(jnp.concatenate([key] * 4, axis=0)))
        value = accs[5][:, 128 * i : 128 * i + 128] * scale
        other = pltpu.roll(value, 64, 1)
        for a, b in ((value, other), (other, value)):
            halves = [jnp.where(left, a, zero), jnp.where(left, zero, b)]
            values.append(jnp.concatenate(halves * 2, axis=0).astype(BF16))
    exps = []
    for g in range(4):
        key = keys[g // 2][64 * (g % 2) : 64 * (g % 2) + 64]
        spread = jnp.concatenate([jnp.where(block == h, key, 0.0) for h in range(4)], axis=0)
        query = jnp.concatenate(
            [rope(accs[g][:, 128 * i : 128 * i + 128]) for i in range(2)], axis=1
        )
        scores = jnp.dot(query.astype(BF16), spread.astype(BF16), preferred_element_type=F32)
        exps.append(jnp.where(mask, jnp.exp(scores * 0.125), 0.0))
    exps = jnp.concatenate(exps, axis=0)
    most = (exps * 0.99609375).astype(BF16)
    rest = (exps - most.astype(F32)).astype(BF16)
    row = lax.broadcasted_iota(jnp.int32, (256, 128), 0) % 128 // SEQ
    col = lax.broadcasted_iota(jnp.int32, (256, 128), 1) // SEQ
    same = jnp.where(row == col, 1.0, 0.0).astype(BF16)
    total = jnp.dot(jnp.concatenate([most, rest], axis=1), same, preferred_element_type=F32)
    power = jnp.where(total > 1.0, 2.0**-8, 2.0**8)
    probs = (exps * power) * (1.0 / (total * power))
    outs = []
    for g in range(4):
        part = probs[SEQ * g : SEQ * g + SEQ]
        part = jnp.concatenate([jnp.where(left, part, 0.0), jnp.where(left, 0.0, part)], axis=0)
        mixed = jnp.dot(part.astype(BF16), values[g], preferred_element_type=F32).astype(BF16)
        outs += [mixed[:SEQ], mixed[SEQ:]]
    return jnp.concatenate(outs, axis=1)


def kernel(
    rows_ref, ids_ref, gain_ref, wq_ref, wkv_ref, wo_ref, table_ref, out_ref,
    raw_q, raw_kv, raw_o, tables, wa_ref, tall, in_ref, seg_ref, raw_sem, w1, w2, xin, segs, wide, mask, xrecv, xsend, staged, owned,
    z_send, z_recv, ring_send, ring_recv, sib_send, sib_recv, cross_send, cross_recv,
    in_send, in_recv, mask_send, mask_recv, x_send, x_recv, o_send, o_recv,
):
    section, fsdp = lax.axis_index("section"), lax.axis_index("fsdp")
    x, zhi, core = section // 4, (section // 2) % 2, section % 2
    y, zlo = fsdp // 4, fsdp % 4
    z = zhi * 4 + zlo
    side = ((x + 1) // 2) % 2
    layer = jnp.where(x < 2, (z + 7) % 8, 8 + (8 - z) % 8)
    first, last = layer == 0, layer == LAST
    plane = section - core

    def place(at_x, at_z, at_core):
        return at_x * 4 + (at_z // 4) * 2 + at_core, y * 4 + at_z % 4

    def host(of_layer, of_side, at_core):
        early = of_layer < 8
        at_x = jnp.where(early, of_side, 3 - of_side)
        return place(at_x, jnp.where(early, of_layer + 1, 16 - of_layer) % 8, at_core)

    def remote(src, dst, send, recv, to):
        return pltpu.make_async_remote_copy(
            src_ref=src, dst_ref=dst, send_sem=send, recv_sem=recv,
            device_id=to, device_id_type=MESH,
        )

    def is_me(to):
        return (to[0] == section) & (to[1] == fsdp)

    sibling = (plane + 1 - core, fsdp)
    partner = place(jnp.where(x < 2, 1 - x, 5 - x), z, core)
    right = (section, ((y + 1) % 8) * 4 + zlo)
    left = (section, ((y + 7) % 8) * 4 + zlo)

    def arrived(dst, recv):
        remote(dst, dst, z_send.at[0], recv, sibling).wait_recv()

    in_to = host(jnp.int32(0), zlo // 2, zlo % 2)
    own_layer = section
    a_to = host(own_layer, zlo // 2, zlo % 2)
    b_to = host(own_layer, zlo // 2, zlo // 2)
    next_to = host(jnp.minimum(layer + 1, LAST), side, core)
    prev_from = host(jnp.maximum(layer - 1, 0), side, core)
    owner_fsdp = y * 4 + 2 * side + core
    result_from = host(jnp.int32(LAST), zlo // 2, zlo % 2)
    a_from = (layer, y * 4 + 2 * side + core)
    b_from = [(layer, y * 4 + 2 * core + u) for u in range(2)]

    raws = [
        pltpu.make_async_copy(src, dst, raw_sem.at[n])
        for n, (src, dst) in enumerate(
            (
                (wq_ref.at[0], raw_q), (wkv_ref.at[0], raw_kv), (wo_ref.at[0], raw_o),
                (table_ref, tables),
            )
        )
    ]
    for raw in raws:
        raw.start()

    barrier = pltpu.get_barrier_semaphore()

    def hello(to):
        pl.semaphore_signal(barrier, inc=1, device_id=to, device_id_type=MESH)

    def hello_other(to):
        @pl.when(jnp.logical_not(is_me(to)))
        def _():
            hello(to)

    for to in (right, left, sibling, partner):
        hello(to)

    for to in (a_from, result_from):
        hello_other(to)

    @pl.when(core == side)
    def _():
        for to in b_from:
            hello_other(to)

    @pl.when(jnp.logical_not(first))
    def _():
        hello(prev_from)

    def hello_all(s, carry):
        hello_other((s, owner_fsdp))
        return carry

    @pl.when(first)
    def _():
        lax.fori_loop(0, 16, hello_all, 0)

    def other(to):
        return jnp.where(is_me(to), 0, 1)

    row = lax.broadcasted_iota(jnp.int32, (64, 64), 0)
    col = lax.broadcasted_iota(jnp.int32, (64, 64), 1)
    gains = jnp.sum(
        jnp.where(row == col, gain_ref[...].astype(F32), 0.0), axis=1, keepdims=True
    )
    for i in range(16):
        tall[:, :, i, :] = rows_ref[:, 0, :, 128 * i : 128 * i + 128].astype(F32)
    in_ref[...] = tall[...].astype(BF16)
    row = lax.broadcasted_iota(jnp.int32, (MICRO * 2, 128), 0)
    ids = jnp.zeros((MICRO * 2, 128), jnp.int32)
    for m in range(MICRO):
        for p in range(2):
            ids = jnp.where(row == 2 * m + p, ids_ref[0, p, m], ids)
    seg_ref[...] = ids.astype(F32)
    for raw in raws:
        raw.wait()
    wa_ref[:, :QW] = (raw_q[...].astype(F32) * gains).astype(BF16)
    wa_ref[:, QW:] = (raw_kv[...].astype(F32) * gains).astype(BF16)

    own_share = jnp.where(owner_fsdp == fsdp, 15, 16)
    expected = 4 + other(in_to) + other(a_to) + other(b_to)
    pl.semaphore_wait(barrier, expected + jnp.where(last, own_share, 1))

    def give(src, dst, send, recv, to):
        @pl.when(is_me(to))
        def _():
            pltpu.make_async_copy(src, dst, recv).start()

        @pl.when(jnp.logical_not(is_me(to)))
        def _():
            remote(src, dst, send, recv, to).start()

    def given(src, dst, send, recv, to):
        @pl.when(jnp.logical_not(is_me(to)))
        def _():
            remote(src, dst, send, recv, to).wait_send()

    own_a = (wa_ref, w1.at[y, zlo // 2, zlo % 2], z_send.at[0], z_recv.at[0], a_to)
    own_b = (raw_o, w2.at[y, zlo // 2, zlo % 2], z_send.at[1], z_recv.at[1 + zlo % 2], b_to)
    own_in = [
        (in_ref, xin.at[:, pl.ds(2 * section, 2)], in_send.at[0], in_recv.at[0], in_to),
        (seg_ref, segs.at[section], in_send.at[1], in_recv.at[1], in_to),
    ]

    give(*own_a)
    given(*own_a)
    for copy in own_in + [own_b]:
        give(*copy)

    sends = []

    def send(ref, sems, recv, to):
        copy = remote(ref, ref, sems.at[len([1 for kind, _ in sends if kind is sems])], recv, to)
        copy.start()
        sends.append((sems, copy))

    def ring(ref, direction, step, part):
        recv = ring_recv.at[(direction * 4 + step) * 3 + part]
        send(ref, ring_send, recv, right if direction == 0 else left)

    def cross(ref, column):
        send(ref, cross_send, cross_recv.at[column], partner)

    def across(ref, part):
        send(ref, sib_send, sib_recv.at[part], sibling)

    def column_of(direction, step):
        return (y + (8 - step if direction == 0 else step)) % 8

    def ring_last(column, direction):
        ref = w1.at[column, side, core]
        return remote(
            ref, ref, ring_send.at[15], ring_recv.at[(direction * 4 + 3) * 3],
            right if direction == 0 else left,
        )

    def w1_at(column):
        return w1.at[column, side, core]

    def w2_at(column, u):
        return w2.at[column, core, u]

    def w2_both(column):
        return w2.at[column, core]

    arrived(w1_at(y), z_recv.at[0])
    for direction in range(2):
        ring(w1_at(y), direction, 0, 0)
    cross(w1_at(y), y)
    across(w1_at(y), 0)
    column_b = remote(w2_both(y), w2_both(y), z_send.at[2], z_recv.at[3], partner)

    @pl.when(core == side)
    def _():
        for u in range(2):
            arrived(w2_at(y, u), z_recv.at[1 + u])
        column_b.start()

    @pl.when(core != side)
    def _():
        arrived(w2_both(y), z_recv.at[3])

    for direction in range(2):
        ring(w2_both(y), direction, 0, 1)
    across(w2_both(y), 1)

    def crossed(column):
        ref = w1.at[column, 1 - side, core]
        arrived(ref, cross_recv.at[column])
        across(ref, 0)

    for step in range(1, 4):
        for direction in range(2):
            column = column_of(direction, step)
            arrived(w1_at(column), ring_recv.at[(direction * 4 + step - 1) * 3])
            if step < 3:
                ring(w1_at(column), direction, step, 0)
            else:
                @pl.when(core == direction)
                def _(column=column, direction=direction):
                    ring_last(column, direction).start()
            cross(w1_at(column), column)
            across(w1_at(column), 0)
        for direction in range(2):
            column = column_of(direction, step)
            arrived(w2_both(column), ring_recv.at[(direction * 4 + step - 1) * 3 + 1])
            ring(w2_both(column) if step < 3 else w2_at(column, direction), direction, step, 1)
            across(w2_both(column), 1)
        if step == 1:
            crossed(y)
        else:
            for direction in range(2):
                crossed(column_of(direction, step - 1))
    def local(m, j):
        return pltpu.make_async_copy(xsend.at[m, j], xrecv.at[m, j], x_recv.at[m * CHUNKS + j])

    @pl.when(first)
    def _():
        arrived(xin, in_recv.at[0])
        arrived(segs, in_recv.at[1])
        row = lax.broadcasted_iota(jnp.int32, (SEQ, 128), 0)
        key = lax.broadcasted_iota(jnp.int32, (SEQ, 128), 1) % SEQ
        to = lax.broadcasted_iota(jnp.int32, (SEQ, SEQ), 0)
        source = lax.broadcasted_iota(jnp.int32, (SEQ, SEQ), 1)
        order = jnp.where(to == 2 * (source % 16) + source // 16, 1.0, 0.0).astype(BF16)

        def load(m, carry):
            wide[...] = xin[m].astype(F32)
            for i in range(16):
                xsend[m, i // TILES, :, (i % TILES) * 128 : (i % TILES) * 128 + 128] = wide[:, i, :].astype(BF16)
            for j in range(CHUNKS):
                local(m, j).start()
            return carry

        lax.fori_loop(0, MICRO, load, 0)
        for m in range(MICRO):
            seg = jnp.concatenate([segs[:, 2 * m, :], segs[:, 2 * m + 1, :]], axis=0)
            seg = jnp.dot(order, seg.astype(BF16), preferred_element_type=F32)
            of_key = jnp.sum(jnp.where(row == key, seg, 0.0), axis=0, keepdims=True)
            allowed = (row >= key) & (seg == of_key)
            mask[m] = jnp.where(allowed, 1.0, 0.0).astype(BF16)

    column = (y + 4) % 8
    for direction in range(2):
        @pl.when(core == direction)
        def _(direction=direction):
            arrived(w1_at(column), ring_recv.at[(direction * 4 + 3) * 3])
    cross(w1_at(column), column)
    across(w1_at(column), 0)
    for direction in range(2):
        arrived(w2_at(column, direction), ring_recv.at[(direction * 4 + 3) * 3 + 1])
        across(w2_at(column, direction), 1)
    for direction in range(2):
        crossed(column_of(direction, 3))
    crossed(column)
    arrived(w1.at[:, :, 1 - core], sib_recv.at[0])
    arrived(w2.at[:, 1 - core], sib_recv.at[1])

    @pl.when(jnp.logical_not(first))
    def _():
        arrived(mask, mask_recv)

    mask_copy = remote(mask, mask, mask_send, mask_recv, next_to)

    @pl.when(jnp.logical_not(last))
    def _():
        mask_copy.start()

    def hop(m, j):
        n = m * CHUNKS + j
        return remote(xsend.at[m, j], xrecv.at[m, j], x_send.at[n], x_recv.at[n], next_to)

    def delivery(m, s):
        return remote(
            staged.at[m, pl.ds(2 * s, 2)], owned.at[m], o_send.at[m * 16 + s], o_recv,
            (s, owner_fsdp),
        )

    def keep(m):
        return pltpu.make_async_copy(staged.at[m, pl.ds(2 * section, 2)], owned.at[m], o_recv)

    def one(m, final):
        accs = [None] * 6
        squares = jnp.zeros((SEQ, 1), F32)
        span = 8 // CHUNKS
        for j in range(CHUNKS):
            arrived(xrecv.at[m, j], x_recv.at[m * CHUNKS + j])
            h = xrecv[m, j]
            hf = h.astype(F32)
            squares = squares + jnp.sum(hf * hf, axis=1, keepdims=True)
            for n in (4, 5, 0, 1, 2, 3):
                weight = w1[span * j : span * (j + 1), :, :, :, 256 * n : 256 * n + 256]
                term = jnp.dot(h, weight.reshape(CHUNK, 256), preferred_element_type=F32)
                accs[n] = term if accs[n] is None else accs[n] + term
        attended = attention(accs, squares, tables[0], tables[1], mask[m].astype(F32) > 0.5)
        for j in range(CHUNKS):
            weight = w2[:, :, :, :, j * CHUNK : (j + 1) * CHUNK].reshape(QW, CHUNK)
            update = jnp.dot(attended, weight, preferred_element_type=F32)
            h = xrecv[m, j].astype(F32) + update
            if final:
                for i in range(TILES):
                    wide[:, TILES * j + i, :] = h[:, 128 * i : 128 * i + 128]
            else:
                xsend[m, j] = h.astype(BF16)
                hop(m, j).start()

        if final:
            staged[m] = wide[...].astype(BF16)

            def hand(s, carry):
                mine = (s == section) & (owner_fsdp == fsdp)

                @pl.when(mine)
                def _():
                    keep(m).start()

                @pl.when(jnp.logical_not(mine))
                def _():
                    delivery(m, s).start()

                return carry

            lax.fori_loop(0, 16, hand, 0)

    def run(final):
        def step(m, carry):
            one(m, final)
            return carry

        lax.fori_loop(0, MICRO, step, 0)

    @pl.when(last)
    def _():
        run(True)

    @pl.when(jnp.logical_not(last))
    def _():
        run(False)

    arrived(owned, o_recv)
    out_ref[...] = owned[...]

    for copy in own_in + [own_b]:
        given(*copy)

    @pl.when(core == side)
    def _():
        column_b.wait_send()

    for _, copy in sends:
        copy.wait_send()
    for direction in range(2):
        @pl.when(core == direction)
        def _(direction=direction):
            ring_last(column_of(direction, 3), direction).wait_send()

    @pl.when(jnp.logical_not(last))
    def _():
        mask_copy.wait_send()

        def drain(n, carry):
            hop(n // CHUNKS, n % CHUNKS).wait_send()
            return carry

        lax.fori_loop(0, MICRO * CHUNKS, drain, 0)

    @pl.when(last)
    def _():
        def drain(n, carry):
            @pl.when(jnp.logical_not((n % 16 == section) & (owner_fsdp == fsdp)))
            def _():
                delivery(n // 16, n % 16).wait_send()

            return carry

        lax.fori_loop(0, MICRO * 16, drain, 0)


def shards(inputs, segments, norm_gains, w_query, w_keyval, w_output):
    vmem = pl.BlockSpec(memory_space=pltpu.VMEM)
    hbm = pl.BlockSpec(memory_space=pltpu.HBM)
    smem = pl.BlockSpec(memory_space=pltpu.SMEM)
    dma = pltpu.SemaphoreType.DMA
    hops = MICRO * CHUNKS
    out = pl.pallas_call(
        kernel,
        out_shape=jax.ShapeDtypeStruct((MICRO, 2, 16, 128), BF16),
        in_specs=[vmem, smem, vmem, hbm, hbm, hbm, hbm],
        out_specs=vmem,
        scratch_shapes=[
            pltpu.VMEM((64, QW), BF16),
            pltpu.VMEM((64, QKV - QW), BF16),
            pltpu.VMEM((32, WIDTH), BF16),
            pltpu.VMEM((2, SEQ, 128), F32),
            pltpu.VMEM((64, QKV), BF16),
            pltpu.VMEM((MICRO, 2, 16, 128), F32),
            pltpu.VMEM((MICRO, 2, 16, 128), BF16),
            pltpu.VMEM((MICRO * 2, 128), F32),
            dma((4,)),
            pltpu.VMEM((8, 2, 2, 64, QKV), BF16),
            pltpu.VMEM((8, 2, 2, 32, WIDTH), BF16),
            pltpu.VMEM((MICRO, SEQ, 16, 128), BF16),
            pltpu.VMEM((16, MICRO * 2, 128), F32),
            pltpu.VMEM((SEQ, 16, 128), F32),
            pltpu.VMEM((MICRO, SEQ, 128), BF16),
            pltpu.VMEM((MICRO, CHUNKS, SEQ, CHUNK), BF16),
            pltpu.VMEM((MICRO, CHUNKS, SEQ, CHUNK), BF16),
            pltpu.VMEM((MICRO, SEQ, 16, 128), BF16),
            pltpu.VMEM((MICRO, 2, 16, 128), BF16),
            dma((3,)), dma((4,)), dma((16,)), dma((24,)), dma((32,)), dma((2,)), dma((8,)), dma((8,)),
            dma((2,)), dma((2,)), dma, dma, dma((hops,)), dma((hops,)), dma((64,)), dma,
        ],
        compiler_params=pltpu.CompilerParams(
            collective_id=0, has_side_effects=True, vmem_limit_bytes=63 * 1024 * 1024
        ),
        name="stack",
    )(
        inputs, jnp.transpose(segments, (1, 2, 0)), norm_gains, w_query, w_keyval, w_output,
        jnp.asarray(np.stack(rope_tables())),
    )
    return out.reshape(MICRO, 1, 2, WIDTH)


def solution(mesh):
    return jax.shard_map(
        shards,
        mesh=mesh,
        in_specs=(
            P(None, "fsdp", "section", None),
            P(None, "fsdp", "section"),
            P("section", "fsdp"),
            P("section", "fsdp", None),
            P("section", "fsdp", None),
            P("section", "fsdp", None),
        ),
        out_specs=P(None, "fsdp", "section", None),
        check_vma=False,
    )
```

```python
import jax
import jax.numpy as jnp
import numpy as np
from jax import lax
from jax.experimental import pallas as pl
from jax.experimental.pallas import tpu as pltpu
from jax.sharding import PartitionSpec as P

MESH = pl.DeviceIdType.MESH
BF16 = jnp.bfloat16
F32 = jnp.float32
EPSILON = 1e-05
THETA = 500000.0
SEQ = 32
MICRO = 4
WIDTH = 2048
CHUNKS = 4
CHUNK = WIDTH // CHUNKS
TILES = CHUNK // 128
QW = 1024
KW = 256
QKV = 1536
LAST = 15


def rope_tables():
    position = np.arange(SEQ, dtype=np.float32)
    freq = (THETA ** (-np.arange(32, dtype=np.float32) * 2.0 / 64)).astype(np.float32)
    angle = (position[:, None] * freq[None, :]).astype(np.float32)
    c, s = np.cos(angle), np.sin(angle)
    return (
        np.concatenate([c, c, c, c], 1).astype(np.float32),
        np.concatenate([-s, s, -s, s], 1).astype(np.float32),
    )


def attention(accs, squares, cosine, sine, mask):
    scale = lax.rsqrt(squares * (1.0 / WIDTH) + EPSILON)
    cosine, sine = cosine * scale, sine * scale
    lane = lax.broadcasted_iota(jnp.int32, (SEQ, 128), 1)
    low, left = (lane & 63) < 32, lane < 64

    def rope(tile):
        swapped = jnp.where(low, pltpu.roll(tile, 96, 1), pltpu.roll(tile, 32, 1))
        return tile * cosine + swapped * sine

    zero = jnp.zeros((SEQ, 128), F32)
    block = lax.broadcasted_iota(jnp.int32, (64, 128), 1) // SEQ
    keys, values = [], []
    for i in range(2):
        key = rope(accs[4][:, 128 * i : 128 * i + 128])
        keys.append(jnp.transpose(jnp.concatenate([key] * 4, axis=0)))
        value = accs[5][:, 128 * i : 128 * i + 128] * scale
        other = pltpu.roll(value, 64, 1)
        for a, b in ((value, other), (other, value)):
            halves = [jnp.where(left, a, zero), jnp.where(left, zero, b)]
            values.append(jnp.concatenate(halves * 2, axis=0).astype(BF16))
    exps = []
    for g in range(4):
        key = keys[g // 2][64 * (g % 2) : 64 * (g % 2) + 64]
        spread = jnp.concatenate([jnp.where(block == h, key, 0.0) for h in range(4)], axis=0)
        query = jnp.concatenate(
            [rope(accs[g][:, 128 * i : 128 * i + 128]) for i in range(2)], axis=1
        )
        scores = jnp.dot(query.astype(BF16), spread.astype(BF16), preferred_element_type=F32)
        exps.append(jnp.where(mask, jnp.exp(scores * 0.125), 0.0))
    exps = jnp.concatenate(exps, axis=0)
    most = (exps * 0.99609375).astype(BF16)
    rest = (exps - most.astype(F32)).astype(BF16)
    row = lax.broadcasted_iota(jnp.int32, (256, 128), 0) % 128 // SEQ
    col = lax.broadcasted_iota(jnp.int32, (256, 128), 1) // SEQ
    same = jnp.where(row == col, 1.0, 0.0).astype(BF16)
    total = jnp.dot(jnp.concatenate([most, rest], axis=1), same, preferred_element_type=F32)
    power = jnp.where(total > 1.0, 2.0**-8, 2.0**8)
    probs = (exps * power) * (1.0 / (total * power))
    outs = []
    for g in range(4):
        part = probs[SEQ * g : SEQ * g + SEQ]
        part = jnp.concatenate([jnp.where(left, part, 0.0), jnp.where(left, 0.0, part)], axis=0)
        mixed = jnp.dot(part.astype(BF16), values[g], preferred_element_type=F32).astype(BF16)
        outs += [mixed[:SEQ], mixed[SEQ:]]
    return jnp.concatenate(outs, axis=1)


def kernel(
    rows_ref, ids_ref, gain_ref, wq_ref, wkv_ref, wo_ref, table_ref, out_ref,
    raw_q, raw_kv, raw_o, tables, wa_ref, tall, in_ref, seg_ref, raw_sem, w1, w2, xin, segs, wide, mask, xrecv, xsend, staged, owned,
    z_send, z_recv, ring_send, ring_recv, sib_send, sib_recv, cross_send, cross_recv,
    in_send, in_recv, mask_send, mask_recv, x_send, x_recv, o_send, o_recv,
):
    section, fsdp = lax.axis_index("section"), lax.axis_index("fsdp")
    x, zhi, core = section // 4, (section // 2) % 2, section % 2
    y, zlo = fsdp // 4, fsdp % 4
    z = zhi * 4 + zlo
    side = ((x + 1) // 2) % 2
    layer = jnp.where(x < 2, (z + 7) % 8, 8 + (8 - z) % 8)
    first, last = layer == 0, layer == LAST
    plane = section - core

    def place(at_x, at_z, at_core):
        return at_x * 4 + (at_z // 4) * 2 + at_core, y * 4 + at_z % 4

    def host(of_layer, of_side, at_core):
        early = of_layer < 8
        at_x = jnp.where(early, of_side, 3 - of_side)
        return place(at_x, jnp.where(early, of_layer + 1, 16 - of_layer) % 8, at_core)

    def remote(src, dst, send, recv, to):
        return pltpu.make_async_remote_copy(
            src_ref=src, dst_ref=dst, send_sem=send, recv_sem=recv,
            device_id=to, device_id_type=MESH,
        )

    def is_me(to):
        return (to[0] == section) & (to[1] == fsdp)

    sibling = (plane + 1 - core, fsdp)
    partner = place(jnp.where(x < 2, 1 - x, 5 - x), z, core)
    right = (section, ((y + 1) % 8) * 4 + zlo)
    left = (section, ((y + 7) % 8) * 4 + zlo)

    def arrived(dst, recv):
        remote(dst, dst, z_send.at[0], recv, sibling).wait_recv()

    in_to = host(jnp.int32(0), zlo // 2, zlo % 2)
    own_layer = section
    a_to = host(own_layer, zlo // 2, zlo % 2)
    b_to = host(own_layer, zlo // 2, zlo // 2)
    next_to = host(jnp.minimum(layer + 1, LAST), side, core)
    prev_from = host(jnp.maximum(layer - 1, 0), side, core)
    owner_fsdp = y * 4 + 2 * side + core
    result_from = host(jnp.int32(LAST), zlo // 2, zlo % 2)
    a_from = (layer, y * 4 + 2 * side + core)
    b_from = [(layer, y * 4 + 2 * core + u) for u in range(2)]

    raws = [
        pltpu.make_async_copy(src, dst, raw_sem.at[n])
        for n, (src, dst) in enumerate(
            (
                (wq_ref.at[0], raw_q), (wkv_ref.at[0], raw_kv), (wo_ref.at[0], raw_o),
                (table_ref, tables),
            )
        )
    ]
    for raw in raws:
        raw.start()

    barrier = pltpu.get_barrier_semaphore()

    def hello(to):
        pl.semaphore_signal(barrier, inc=1, device_id=to, device_id_type=MESH)

    def hello_other(to):
        @pl.when(jnp.logical_not(is_me(to)))
        def _():
            hello(to)

    for to in (right, left, sibling, partner):
        hello(to)

    for to in (a_from, result_from):
        hello_other(to)

    @pl.when(core == side)
    def _():
        for to in b_from:
            hello_other(to)

    @pl.when(jnp.logical_not(first))
    def _():
        hello(prev_from)

    def hello_all(s, carry):
        hello_other((s, owner_fsdp))
        return carry

    @pl.when(first)
    def _():
        lax.fori_loop(0, 16, hello_all, 0)

    def other(to):
        return jnp.where(is_me(to), 0, 1)

    row = lax.broadcasted_iota(jnp.int32, (64, 64), 0)
    col = lax.broadcasted_iota(jnp.int32, (64, 64), 1)
    gains = jnp.sum(
        jnp.where(row == col, gain_ref[...].astype(F32), 0.0), axis=1, keepdims=True
    )
    for i in range(16):
        tall[:, :, i, :] = rows_ref[:, 0, :, 128 * i : 128 * i + 128].astype(F32)
    in_ref[...] = tall[...].astype(BF16)
    row = lax.broadcasted_iota(jnp.int32, (MICRO * 2, 128), 0)
    ids = jnp.zeros((MICRO * 2, 128), jnp.int32)
    for m in range(MICRO):
        for p in range(2):
            ids = jnp.where(row == 2 * m + p, ids_ref[0, p, m], ids)
    seg_ref[...] = ids.astype(F32)
    for raw in raws:
        raw.wait()
    wa_ref[:, :QW] = (raw_q[...].astype(F32) * gains).astype(BF16)
    wa_ref[:, QW:] = (raw_kv[...].astype(F32) * gains).astype(BF16)

    own_share = jnp.where(owner_fsdp == fsdp, 15, 16)
    expected = 4 + other(in_to) + other(a_to) + other(b_to)
    pl.semaphore_wait(barrier, expected + jnp.where(last, own_share, 1))

    def give(src, dst, send, recv, to):
        @pl.when(is_me(to))
        def _():
            pltpu.make_async_copy(src, dst, recv).start()

        @pl.when(jnp.logical_not(is_me(to)))
        def _():
            remote(src, dst, send, recv, to).start()

    def given(src, dst, send, recv, to):
        @pl.when(jnp.logical_not(is_me(to)))
        def _():
            remote(src, dst, send, recv, to).wait_send()

    own_a = (wa_ref, w1.at[y, zlo // 2, zlo % 2], z_send.at[0], z_recv.at[0], a_to)
    own_b = (raw_o, w2.at[y, zlo // 2, zlo % 2], z_send.at[1], z_recv.at[1 + zlo % 2], b_to)
    own_in = [
        (in_ref, xin.at[:, pl.ds(2 * section, 2)], in_send.at[0], in_recv.at[0], in_to),
        (seg_ref, segs.at[section], in_send.at[1], in_recv.at[1], in_to),
    ]

    give(*own_a)
    for copy in [own_b] + own_in:
        give(*copy)

    sends = []

    def send(ref, sems, recv, to):
        copy = remote(ref, ref, sems.at[len([1 for kind, _ in sends if kind is sems])], recv, to)
        copy.start()
        sends.append((sems, copy))

    def ring(ref, direction, step, part):
        recv = ring_recv.at[(direction * 4 + step) * 3 + part]
        send(ref, ring_send, recv, right if direction == 0 else left)

    def cross(ref, column):
        send(ref, cross_send, cross_recv.at[column], partner)

    def across(ref, part):
        send(ref, sib_send, sib_recv.at[part], sibling)

    def column_of(direction, step):
        return (y + (8 - step if direction == 0 else step)) % 8

    def ring_last(column, direction):
        ref = w1.at[column, side, core]
        return remote(
            ref, ref, ring_send.at[15], ring_recv.at[(direction * 4 + 3) * 3],
            right if direction == 0 else left,
        )

    def w1_at(column):
        return w1.at[column, side, core]

    def w2_at(column, u):
        return w2.at[column, core, u]

    def w2_both(column):
        return w2.at[column, core]

    arrived(w1_at(y), z_recv.at[0])
    for direction in range(2):
        ring(w1_at(y), direction, 0, 0)
    cross(w1_at(y), y)
    across(w1_at(y), 0)
    column_b = remote(w2_both(y), w2_both(y), z_send.at[2], z_recv.at[3], partner)

    @pl.when(core == side)
    def _():
        for u in range(2):
            arrived(w2_at(y, u), z_recv.at[1 + u])
        column_b.start()

    @pl.when(core != side)
    def _():
        arrived(w2_both(y), z_recv.at[3])

    for direction in range(2):
        ring(w2_both(y), direction, 0, 1)
    across(w2_both(y), 1)

    def crossed(column):
        ref = w1.at[column, 1 - side, core]
        arrived(ref, cross_recv.at[column])
        across(ref, 0)

    for step in range(1, 4):
        for direction in range(2):
            column = column_of(direction, step)
            arrived(w1_at(column), ring_recv.at[(direction * 4 + step - 1) * 3])
            if step < 3:
                ring(w1_at(column), direction, step, 0)
            else:
                @pl.when(core == direction)
                def _(column=column, direction=direction):
                    ring_last(column, direction).start()
            cross(w1_at(column), column)
            across(w1_at(column), 0)
        for direction in range(2):
            column = column_of(direction, step)
            arrived(w2_both(column), ring_recv.at[(direction * 4 + step - 1) * 3 + 1])
            ring(w2_both(column) if step < 3 else w2_at(column, direction), direction, step, 1)
            across(w2_both(column), 1)
    def local(m, j):
        return pltpu.make_async_copy(xsend.at[m, j], xrecv.at[m, j], x_recv.at[m * CHUNKS + j])

    @pl.when(first)
    def _():
        arrived(xin, in_recv.at[0])
        arrived(segs, in_recv.at[1])
        row = lax.broadcasted_iota(jnp.int32, (SEQ, 128), 0)
        key = lax.broadcasted_iota(jnp.int32, (SEQ, 128), 1) % SEQ
        to = lax.broadcasted_iota(jnp.int32, (SEQ, SEQ), 0)
        source = lax.broadcasted_iota(jnp.int32, (SEQ, SEQ), 1)
        order = jnp.where(to == 2 * (source % 16) + source // 16, 1.0, 0.0).astype(BF16)

        def load(m, carry):
            wide[...] = xin[m].astype(F32)
            for i in range(16):
                xsend[m, i // TILES, :, (i % TILES) * 128 : (i % TILES) * 128 + 128] = wide[:, i, :].astype(BF16)
            for j in range(CHUNKS):
                local(m, j).start()
            return carry

        lax.fori_loop(0, MICRO, load, 0)
        for m in range(MICRO):
            seg = jnp.concatenate([segs[:, 2 * m, :], segs[:, 2 * m + 1, :]], axis=0)
            seg = jnp.dot(order, seg.astype(BF16), preferred_element_type=F32)
            of_key = jnp.sum(jnp.where(row == key, seg, 0.0), axis=0, keepdims=True)
            allowed = (row >= key) & (seg == of_key)
            mask[m] = jnp.where(allowed, 1.0, 0.0).astype(BF16)

    column = (y + 4) % 8
    for direction in range(2):
        @pl.when(core == direction)
        def _(direction=direction):
            arrived(w1_at(column), ring_recv.at[(direction * 4 + 3) * 3])
    cross(w1_at(column), column)
    across(w1_at(column), 0)
    for direction in range(2):
        arrived(w2_at(column, direction), ring_recv.at[(direction * 4 + 3) * 3 + 1])
        across(w2_at(column, direction), 1)
    crossed(y)
    for step in range(1, 4):
        for direction in range(2):
            crossed(column_of(direction, step))
    crossed(column)
    arrived(w1.at[:, :, 1 - core], sib_recv.at[0])
    arrived(w2.at[:, 1 - core], sib_recv.at[1])

    @pl.when(jnp.logical_not(first))
    def _():
        arrived(mask, mask_recv)

    mask_copy = remote(mask, mask, mask_send, mask_recv, next_to)

    @pl.when(jnp.logical_not(last))
    def _():
        mask_copy.start()

    def hop(m, j):
        n = m * CHUNKS + j
        return remote(xsend.at[m, j], xrecv.at[m, j], x_send.at[n], x_recv.at[n], next_to)

    def delivery(m, s):
        return remote(
            staged.at[m, pl.ds(2 * s, 2)], owned.at[m], o_send.at[m * 16 + s], o_recv,
            (s, owner_fsdp),
        )

    def keep(m):
        return pltpu.make_async_copy(staged.at[m, pl.ds(2 * section, 2)], owned.at[m], o_recv)

    def one(m, final):
        accs = [None] * 6
        squares = jnp.zeros((SEQ, 1), F32)
        span = 8 // CHUNKS
        for j in range(CHUNKS):
            arrived(xrecv.at[m, j], x_recv.at[m * CHUNKS + j])
            h = xrecv[m, j]
            hf = h.astype(F32)
            squares = squares + jnp.sum(hf * hf, axis=1, keepdims=True)
            for n in (4, 5, 0, 1, 2, 3):
                weight = w1[span * j : span * (j + 1), :, :, :, 256 * n : 256 * n + 256]
                term = jnp.dot(h, weight.reshape(CHUNK, 256), preferred_element_type=F32)
                accs[n] = term if accs[n] is None else accs[n] + term
        attended = attention(accs, squares, tables[0], tables[1], mask[m].astype(F32) > 0.5)
        for j in range(CHUNKS):
            weight = w2[:, :, :, :, j * CHUNK : (j + 1) * CHUNK].reshape(QW, CHUNK)
            update = jnp.dot(attended, weight, preferred_element_type=F32)
            h = xrecv[m, j].astype(F32) + update
            if final:
                for i in range(TILES):
                    wide[:, TILES * j + i, :] = h[:, 128 * i : 128 * i + 128]
            else:
                xsend[m, j] = h.astype(BF16)
                hop(m, j).start()

        if final:
            staged[m] = wide[...].astype(BF16)

            def hand(s, carry):
                mine = (s == section) & (owner_fsdp == fsdp)

                @pl.when(mine)
                def _():
                    keep(m).start()

                @pl.when(jnp.logical_not(mine))
                def _():
                    delivery(m, s).start()

                return carry

            lax.fori_loop(0, 16, hand, 0)

    def run(final):
        def step(m, carry):
            one(m, final)
            return carry

        lax.fori_loop(0, MICRO, step, 0)

    @pl.when(last)
    def _():
        run(True)

    @pl.when(jnp.logical_not(last))
    def _():
        run(False)

    arrived(owned, o_recv)
    out_ref[...] = owned[...]

    for copy in own_in + [own_a, own_b]:
        given(*copy)

    @pl.when(core == side)
    def _():
        column_b.wait_send()

    for _, copy in sends:
        copy.wait_send()
    for direction in range(2):
        @pl.when(core == direction)
        def _(direction=direction):
            ring_last(column_of(direction, 3), direction).wait_send()

    @pl.when(jnp.logical_not(last))
    def _():
        mask_copy.wait_send()

        def drain(n, carry):
            hop(n // CHUNKS, n % CHUNKS).wait_send()
            return carry

        lax.fori_loop(0, MICRO * CHUNKS, drain, 0)

    @pl.when(last)
    def _():
        def drain(n, carry):
            @pl.when(jnp.logical_not((n % 16 == section) & (owner_fsdp == fsdp)))
            def _():
                delivery(n // 16, n % 16).wait_send()

            return carry

        lax.fori_loop(0, MICRO * 16, drain, 0)


def shards(inputs, segments, norm_gains, w_query, w_keyval, w_output):
    vmem = pl.BlockSpec(memory_space=pltpu.VMEM)
    hbm = pl.BlockSpec(memory_space=pltpu.HBM)
    smem = pl.BlockSpec(memory_space=pltpu.SMEM)
    dma = pltpu.SemaphoreType.DMA
    hops = MICRO * CHUNKS
    out = pl.pallas_call(
        kernel,
        out_shape=jax.ShapeDtypeStruct((MICRO, 2, 16, 128), BF16),
        in_specs=[vmem, smem, vmem, hbm, hbm, hbm, hbm],
        out_specs=vmem,
        scratch_shapes=[
            pltpu.VMEM((64, QW), BF16),
            pltpu.VMEM((64, QKV - QW), BF16),
            pltpu.VMEM((32, WIDTH), BF16),
            pltpu.VMEM((2, SEQ, 128), F32),
            pltpu.VMEM((64, QKV), BF16),
            pltpu.VMEM((MICRO, 2, 16, 128), F32),
            pltpu.VMEM((MICRO, 2, 16, 128), BF16),
            pltpu.VMEM((MICRO * 2, 128), F32),
            dma((4,)),
            pltpu.VMEM((8, 2, 2, 64, QKV), BF16),
            pltpu.VMEM((8, 2, 2, 32, WIDTH), BF16),
            pltpu.VMEM((MICRO, SEQ, 16, 128), BF16),
            pltpu.VMEM((16, MICRO * 2, 128), F32),
            pltpu.VMEM((SEQ, 16, 128), F32),
            pltpu.VMEM((MICRO, SEQ, 128), BF16),
            pltpu.VMEM((MICRO, CHUNKS, SEQ, CHUNK), BF16),
            pltpu.VMEM((MICRO, CHUNKS, SEQ, CHUNK), BF16),
            pltpu.VMEM((MICRO, SEQ, 16, 128), BF16),
            pltpu.VMEM((MICRO, 2, 16, 128), BF16),
            dma((3,)), dma((4,)), dma((16,)), dma((24,)), dma((32,)), dma((2,)), dma((8,)), dma((8,)),
            dma((2,)), dma((2,)), dma, dma, dma((hops,)), dma((hops,)), dma((64,)), dma,
        ],
        compiler_params=pltpu.CompilerParams(
            collective_id=0, has_side_effects=True, vmem_limit_bytes=63 * 1024 * 1024
        ),
        name="stack",
    )(
        inputs, jnp.transpose(segments, (1, 2, 0)), norm_gains, w_query, w_keyval, w_output,
        jnp.asarray(np.stack(rope_tables())),
    )
    return out.reshape(MICRO, 1, 2, WIDTH)


def solution(mesh):
    return jax.shard_map(
        shards,
        mesh=mesh,
        in_specs=(
            P(None, "fsdp", "section", None),
            P(None, "fsdp", "section"),
            P("section", "fsdp"),
            P("section", "fsdp", None),
            P("section", "fsdp", None),
            P("section", "fsdp", None),
        ),
        out_specs=P(None, "fsdp", "section", None),
        check_vma=False,
    )
```

```python
import jax
import jax.numpy as jnp
import numpy as np
from jax import lax
from jax.experimental import pallas as pl
from jax.experimental.pallas import tpu as pltpu
from jax.sharding import PartitionSpec as P

MESH = pl.DeviceIdType.MESH
BF16 = jnp.bfloat16
F32 = jnp.float32
EPSILON = 1e-05
THETA = 500000.0
SEQ = 32
MICRO = 4
WIDTH = 2048
CHUNKS = 4
CHUNK = WIDTH // CHUNKS
TILES = CHUNK // 128
QW = 1024
KW = 256
QKV = 1536
LAST = 15


def rope_tables():
    position = np.arange(SEQ, dtype=np.float32)
    freq = (THETA ** (-np.arange(32, dtype=np.float32) * 2.0 / 64)).astype(np.float32)
    angle = (position[:, None] * freq[None, :]).astype(np.float32)
    c, s = np.cos(angle), np.sin(angle)
    return (
        np.concatenate([c, c, c, c], 1).astype(np.float32),
        np.concatenate([-s, s, -s, s], 1).astype(np.float32),
    )


def attention(accs, squares, cosine, sine, mask):
    scale = lax.rsqrt(squares * (1.0 / WIDTH) + EPSILON)
    cosine, sine = cosine * scale, sine * scale
    lane = lax.broadcasted_iota(jnp.int32, (SEQ, 128), 1)
    low, left = (lane & 63) < 32, lane < 64

    def rope(tile):
        swapped = jnp.where(low, pltpu.roll(tile, 96, 1), pltpu.roll(tile, 32, 1))
        return tile * cosine + swapped * sine

    zero = jnp.zeros((SEQ, 128), F32)
    block = lax.broadcasted_iota(jnp.int32, (64, 128), 1) // SEQ
    keys, values = [], []
    for i in range(2):
        key = rope(accs[4][:, 128 * i : 128 * i + 128])
        keys.append(jnp.transpose(jnp.concatenate([key] * 4, axis=0)))
        value = accs[5][:, 128 * i : 128 * i + 128] * scale
        other = pltpu.roll(value, 64, 1)
        for a, b in ((value, other), (other, value)):
            halves = [jnp.where(left, a, zero), jnp.where(left, zero, b)]
            values.append(jnp.concatenate(halves * 2, axis=0).astype(BF16))
    exps = []
    for g in range(4):
        key = keys[g // 2][64 * (g % 2) : 64 * (g % 2) + 64]
        spread = jnp.concatenate([jnp.where(block == h, key, 0.0) for h in range(4)], axis=0)
        query = jnp.concatenate(
            [rope(accs[g][:, 128 * i : 128 * i + 128]) for i in range(2)], axis=1
        )
        scores = jnp.dot(query.astype(BF16), spread.astype(BF16), preferred_element_type=F32)
        exps.append(jnp.where(mask, jnp.exp(scores * 0.125), 0.0))
    exps = jnp.concatenate(exps, axis=0)
    most = (exps * 0.99609375).astype(BF16)
    rest = (exps - most.astype(F32)).astype(BF16)
    row = lax.broadcasted_iota(jnp.int32, (256, 128), 0) % 128 // SEQ
    col = lax.broadcasted_iota(jnp.int32, (256, 128), 1) // SEQ
    same = jnp.where(row == col, 1.0, 0.0).astype(BF16)
    total = jnp.dot(jnp.concatenate([most, rest], axis=1), same, preferred_element_type=F32)
    power = jnp.where(total > 1.0, 2.0**-8, 2.0**8)
    probs = (exps * power) * (1.0 / (total * power))
    outs = []
    for g in range(4):
        part = probs[SEQ * g : SEQ * g + SEQ]
        part = jnp.concatenate([jnp.where(left, part, 0.0), jnp.where(left, 0.0, part)], axis=0)
        mixed = jnp.dot(part.astype(BF16), values[g], preferred_element_type=F32).astype(BF16)
        outs += [mixed[:SEQ], mixed[SEQ:]]
    return jnp.concatenate(outs, axis=1)


def kernel(
    rows_ref, ids_ref, gain_ref, wq_ref, wkv_ref, wo_ref, table_ref, out_ref,
    raw_q, raw_kv, raw_o, tables, wa_ref, tall, in_ref, seg_ref, raw_sem, w1, w2, xin, segs, wide, mask, xrecv, xsend, staged, owned,
    z_send, z_recv, ring_send, ring_recv, sib_send, sib_recv, cross_send, cross_recv,
    in_send, in_recv, mask_send, mask_recv, x_send, x_recv, o_send, o_recv,
):
    section, fsdp = lax.axis_index("section"), lax.axis_index("fsdp")
    x, zhi, core = section // 4, (section // 2) % 2, section % 2
    y, zlo = fsdp // 4, fsdp % 4
    z = zhi * 4 + zlo
    side = ((x + 1) // 2) % 2
    layer = jnp.where(x < 2, (z + 7) % 8, 8 + (8 - z) % 8)
    first, last = layer == 0, layer == LAST
    plane = section - core

    def place(at_x, at_z, at_core):
        return at_x * 4 + (at_z // 4) * 2 + at_core, y * 4 + at_z % 4

    def host(of_layer, of_side, at_core):
        early = of_layer < 8
        at_x = jnp.where(early, of_side, 3 - of_side)
        return place(at_x, jnp.where(early, of_layer + 1, 16 - of_layer) % 8, at_core)

    def remote(src, dst, send, recv, to):
        return pltpu.make_async_remote_copy(
            src_ref=src, dst_ref=dst, send_sem=send, recv_sem=recv,
            device_id=to, device_id_type=MESH,
        )

    def is_me(to):
        return (to[0] == section) & (to[1] == fsdp)

    sibling = (plane + 1 - core, fsdp)
    partner = place(jnp.where(x < 2, 1 - x, 5 - x), z, core)
    right = (section, ((y + 1) % 8) * 4 + zlo)
    left = (section, ((y + 7) % 8) * 4 + zlo)

    def arrived(dst, recv):
        remote(dst, dst, z_send.at[0], recv, sibling).wait_recv()

    in_to = host(jnp.int32(0), zlo // 2, zlo % 2)
    own_layer = section
    a_to = host(own_layer, zlo // 2, zlo % 2)
    b_to = host(own_layer, zlo // 2, zlo // 2)
    next_to = host(jnp.minimum(layer + 1, LAST), side, core)
    prev_from = host(jnp.maximum(layer - 1, 0), side, core)
    owner_fsdp = y * 4 + 2 * side + core
    result_from = host(jnp.int32(LAST), zlo // 2, zlo % 2)
    a_from = (layer, y * 4 + 2 * side + core)
    b_from = [(layer, y * 4 + 2 * core + u) for u in range(2)]

    raws = [
        pltpu.make_async_copy(src, dst, raw_sem.at[n])
        for n, (src, dst) in enumerate(
            (
                (wq_ref.at[0], raw_q), (wkv_ref.at[0], raw_kv), (wo_ref.at[0], raw_o),
                (table_ref, tables),
            )
        )
    ]
    for raw in raws:
        raw.start()

    barrier = pltpu.get_barrier_semaphore()

    def hello(to):
        pl.semaphore_signal(barrier, inc=1, device_id=to, device_id_type=MESH)

    def hello_other(to):
        @pl.when(jnp.logical_not(is_me(to)))
        def _():
            hello(to)

    for to in (right, left, sibling, partner):
        hello(to)

    for to in (a_from, result_from):
        hello_other(to)

    @pl.when(core == side)
    def _():
        for to in b_from:
            hello_other(to)

    @pl.when(jnp.logical_not(first))
    def _():
        hello(prev_from)

    def hello_all(s, carry):
        hello_other((s, owner_fsdp))
        return carry

    @pl.when(first)
    def _():
        lax.fori_loop(0, 16, hello_all, 0)

    def other(to):
        return jnp.where(is_me(to), 0, 1)

    row = lax.broadcasted_iota(jnp.int32, (64, 64), 0)
    col = lax.broadcasted_iota(jnp.int32, (64, 64), 1)
    gains = jnp.sum(
        jnp.where(row == col, gain_ref[...].astype(F32), 0.0), axis=1, keepdims=True
    )
    for i in range(16):
        tall[:, :, i, :] = rows_ref[:, 0, :, 128 * i : 128 * i + 128].astype(F32)
    in_ref[...] = tall[...].astype(BF16)
    row = lax.broadcasted_iota(jnp.int32, (MICRO * 2, 128), 0)
    ids = jnp.zeros((MICRO * 2, 128), jnp.int32)
    for m in range(MICRO):
        for p in range(2):
            ids = jnp.where(row == 2 * m + p, ids_ref[0, p, m], ids)
    seg_ref[...] = ids.astype(F32)
    for raw in raws:
        raw.wait()
    wa_ref[:, :QW] = (raw_q[...].astype(F32) * gains).astype(BF16)
    wa_ref[:, QW:] = (raw_kv[...].astype(F32) * gains).astype(BF16)

    own_share = jnp.where(owner_fsdp == fsdp, 15, 16)
    expected = 4 + other(in_to) + other(a_to) + other(b_to)
    pl.semaphore_wait(barrier, expected + jnp.where(last, own_share, 1))

    def give(src, dst, send, recv, to):
        @pl.when(is_me(to))
        def _():
            pltpu.make_async_copy(src, dst, recv).start()

        @pl.when(jnp.logical_not(is_me(to)))
        def _():
            remote(src, dst, send, recv, to).start()

    def given(src, dst, send, recv, to):
        @pl.when(jnp.logical_not(is_me(to)))
        def _():
            remote(src, dst, send, recv, to).wait_send()

    own_a = (wa_ref, w1.at[y, zlo // 2, zlo % 2], z_send.at[0], z_recv.at[0], a_to)
    own_b = (raw_o, w2.at[y, zlo // 2, zlo % 2], z_send.at[1], z_recv.at[1 + zlo % 2], b_to)
    own_in = [
        (in_ref, xin.at[:, pl.ds(2 * section, 2)], in_send.at[0], in_recv.at[0], in_to),
        (seg_ref, segs.at[section], in_send.at[1], in_recv.at[1], in_to),
    ]

    give(*own_a)
    for copy in [own_b] + own_in:
        give(*copy)

    sends = []

    def send(ref, sems, recv, to):
        copy = remote(ref, ref, sems.at[len([1 for kind, _ in sends if kind is sems])], recv, to)
        copy.start()
        sends.append((sems, copy))

    def ring(ref, direction, step, part):
        recv = ring_recv.at[(direction * 4 + step) * 3 + part]
        send(ref, ring_send, recv, right if direction == 0 else left)

    def cross(ref, column):
        send(ref, cross_send, cross_recv.at[column], partner)

    def across(ref, part):
        send(ref, sib_send, sib_recv.at[part], sibling)

    def column_of(direction, step):
        return (y + (8 - step if direction == 0 else step)) % 8

    def ring_last(column, direction):
        ref = w1.at[column, side, core]
        return remote(
            ref, ref, ring_send.at[15], ring_recv.at[(direction * 4 + 3) * 3],
            right if direction == 0 else left,
        )

    def w1_at(column):
        return w1.at[column, side, core]

    def w2_at(column, u):
        return w2.at[column, core, u]

    def w2_both(column):
        return w2.at[column, core]

    arrived(w1_at(y), z_recv.at[0])
    for direction in range(2):
        ring(w1_at(y), direction, 0, 0)
    cross(w1_at(y), y)
    across(w1_at(y), 0)
    column_b = remote(w2_both(y), w2_both(y), z_send.at[2], z_recv.at[3], partner)

    @pl.when(core == side)
    def _():
        for u in range(2):
            arrived(w2_at(y, u), z_recv.at[1 + u])
        column_b.start()

    @pl.when(core != side)
    def _():
        arrived(w2_both(y), z_recv.at[3])

    for direction in range(2):
        ring(w2_both(y), direction, 0, 1)
    across(w2_both(y), 1)

    def crossed(column):
        ref = w1.at[column, 1 - side, core]
        arrived(ref, cross_recv.at[column])
        across(ref, 0)

    for step in range(1, 4):
        for direction in range(2):
            column = column_of(direction, step)
            arrived(w1_at(column), ring_recv.at[(direction * 4 + step - 1) * 3])
            if step < 3:
                ring(w1_at(column), direction, step, 0)
            else:
                @pl.when(core == direction)
                def _(column=column, direction=direction):
                    ring_last(column, direction).start()
            cross(w1_at(column), column)
            across(w1_at(column), 0)
        for direction in range(2):
            column = column_of(direction, step)
            arrived(w2_both(column), ring_recv.at[(direction * 4 + step - 1) * 3 + 1])
            ring(w2_both(column) if step < 3 else w2_at(column, direction), direction, step, 1)
            across(w2_both(column), 1)
    def local(m, j):
        return pltpu.make_async_copy(xsend.at[m, j], xrecv.at[m, j], x_recv.at[m * CHUNKS + j])

    def load_all():
        arrived(xin, in_recv.at[0])
        arrived(segs, in_recv.at[1])
        row = lax.broadcasted_iota(jnp.int32, (SEQ, 128), 0)
        key = lax.broadcasted_iota(jnp.int32, (SEQ, 128), 1) % SEQ
        to = lax.broadcasted_iota(jnp.int32, (SEQ, SEQ), 0)
        source = lax.broadcasted_iota(jnp.int32, (SEQ, SEQ), 1)
        order = jnp.where(to == 2 * (source % 16) + source // 16, 1.0, 0.0).astype(BF16)

        def load(m, carry):
            wide[...] = xin[m].astype(F32)
            for i in range(16):
                xsend[m, i // TILES, :, (i % TILES) * 128 : (i % TILES) * 128 + 128] = wide[:, i, :].astype(BF16)
            for j in range(CHUNKS):
                local(m, j).start()
            return carry

        lax.fori_loop(0, MICRO, load, 0)
        for m in range(MICRO):
            seg = jnp.concatenate([segs[:, 2 * m, :], segs[:, 2 * m + 1, :]], axis=0)
            seg = jnp.dot(order, seg.astype(BF16), preferred_element_type=F32)
            of_key = jnp.sum(jnp.where(row == key, seg, 0.0), axis=0, keepdims=True)
            allowed = (row >= key) & (seg == of_key)
            mask[m] = jnp.where(allowed, 1.0, 0.0).astype(BF16)

    @pl.when(first & (core == 0))
    def _():
        load_all()

    column = (y + 4) % 8
    for direction in range(2):
        @pl.when(core == direction)
        def _(direction=direction):
            arrived(w1_at(column), ring_recv.at[(direction * 4 + 3) * 3])
    cross(w1_at(column), column)
    across(w1_at(column), 0)
    for direction in range(2):
        arrived(w2_at(column, direction), ring_recv.at[(direction * 4 + 3) * 3 + 1])
        across(w2_at(column, direction), 1)
    crossed(y)
    for step in range(1, 4):
        for direction in range(2):
            crossed(column_of(direction, step))
    crossed(column)
    arrived(w1.at[:, :, 1 - core], sib_recv.at[0])
    arrived(w2.at[:, 1 - core], sib_recv.at[1])

    @pl.when(first & (core == 1))
    def _():
        load_all()

    @pl.when(jnp.logical_not(first))
    def _():
        arrived(mask, mask_recv)

    mask_copy = remote(mask, mask, mask_send, mask_recv, next_to)

    @pl.when(jnp.logical_not(last))
    def _():
        mask_copy.start()

    def hop(m, j):
        n = m * CHUNKS + j
        return remote(xsend.at[m, j], xrecv.at[m, j], x_send.at[n], x_recv.at[n], next_to)

    def delivery(m, s):
        return remote(
            staged.at[m, pl.ds(2 * s, 2)], owned.at[m], o_send.at[m * 16 + s], o_recv,
            (s, owner_fsdp),
        )

    def keep(m):
        return pltpu.make_async_copy(staged.at[m, pl.ds(2 * section, 2)], owned.at[m], o_recv)

    def one(m, final):
        accs = [None] * 6
        squares = jnp.zeros((SEQ, 1), F32)
        span = 8 // CHUNKS
        for j in range(CHUNKS):
            arrived(xrecv.at[m, j], x_recv.at[m * CHUNKS + j])
            h = xrecv[m, j]
            hf = h.astype(F32)
            squares = squares + jnp.sum(hf * hf, axis=1, keepdims=True)
            for n in (4, 5, 0, 1, 2, 3):
                weight = w1[span * j : span * (j + 1), :, :, :, 256 * n : 256 * n + 256]
                term = jnp.dot(h, weight.reshape(CHUNK, 256), preferred_element_type=F32)
                accs[n] = term if accs[n] is None else accs[n] + term
        attended = attention(accs, squares, tables[0], tables[1], mask[m].astype(F32) > 0.5)
        for j in range(CHUNKS):
            weight = w2[:, :, :, :, j * CHUNK : (j + 1) * CHUNK].reshape(QW, CHUNK)
            update = jnp.dot(attended, weight, preferred_element_type=F32)
            h = xrecv[m, j].astype(F32) + update
            if final:
                for i in range(TILES):
                    wide[:, TILES * j + i, :] = h[:, 128 * i : 128 * i + 128]
            else:
                xsend[m, j] = h.astype(BF16)
                hop(m, j).start()

        if final:
            staged[m] = wide[...].astype(BF16)

            for s in range(16):
                mine = (section == s) & (owner_fsdp == fsdp)

                @pl.when(mine)
                def _():
                    keep(m).start()

                @pl.when(jnp.logical_not(mine))
                def _(s=s):
                    delivery(m, s).start()

    def run(final):
        def step(m, carry):
            one(m, final)
            return carry

        lax.fori_loop(0, MICRO, step, 0)

    @pl.when(last)
    def _():
        run(True)

    @pl.when(jnp.logical_not(last))
    def _():
        run(False)

    arrived(owned, o_recv)
    out_ref[...] = owned[...]

    for copy in own_in + [own_a, own_b]:
        given(*copy)

    @pl.when(core == side)
    def _():
        column_b.wait_send()

    for _, copy in sends:
        copy.wait_send()
    for direction in range(2):
        @pl.when(core == direction)
        def _(direction=direction):
            ring_last(column_of(direction, 3), direction).wait_send()

    @pl.when(jnp.logical_not(last))
    def _():
        mask_copy.wait_send()

        def drain(n, carry):
            hop(n // CHUNKS, n % CHUNKS).wait_send()
            return carry

        lax.fori_loop(0, MICRO * CHUNKS, drain, 0)

    @pl.when(last)
    def _():
        def drain(n, carry):
            @pl.when(jnp.logical_not((n % 16 == section) & (owner_fsdp == fsdp)))
            def _():
                delivery(n // 16, n % 16).wait_send()

            return carry

        lax.fori_loop(0, MICRO * 16, drain, 0)


def shards(inputs, segments, norm_gains, w_query, w_keyval, w_output):
    vmem = pl.BlockSpec(memory_space=pltpu.VMEM)
    hbm = pl.BlockSpec(memory_space=pltpu.HBM)
    smem = pl.BlockSpec(memory_space=pltpu.SMEM)
    dma = pltpu.SemaphoreType.DMA
    hops = MICRO * CHUNKS
    out = pl.pallas_call(
        kernel,
        out_shape=jax.ShapeDtypeStruct((MICRO, 2, 16, 128), BF16),
        in_specs=[vmem, smem, vmem, hbm, hbm, hbm, hbm],
        out_specs=vmem,
        scratch_shapes=[
            pltpu.VMEM((64, QW), BF16),
            pltpu.VMEM((64, QKV - QW), BF16),
            pltpu.VMEM((32, WIDTH), BF16),
            pltpu.VMEM((2, SEQ, 128), F32),
            pltpu.VMEM((64, QKV), BF16),
            pltpu.VMEM((MICRO, 2, 16, 128), F32),
            pltpu.VMEM((MICRO, 2, 16, 128), BF16),
            pltpu.VMEM((MICRO * 2, 128), F32),
            dma((4,)),
            pltpu.VMEM((8, 2, 2, 64, QKV), BF16),
            pltpu.VMEM((8, 2, 2, 32, WIDTH), BF16),
            pltpu.VMEM((MICRO, SEQ, 16, 128), BF16),
            pltpu.VMEM((16, MICRO * 2, 128), F32),
            pltpu.VMEM((SEQ, 16, 128), F32),
            pltpu.VMEM((MICRO, SEQ, 128), BF16),
            pltpu.VMEM((MICRO, CHUNKS, SEQ, CHUNK), BF16),
            pltpu.VMEM((MICRO, CHUNKS, SEQ, CHUNK), BF16),
            pltpu.VMEM((MICRO, SEQ, 16, 128), BF16),
            pltpu.VMEM((MICRO, 2, 16, 128), BF16),
            dma((3,)), dma((4,)), dma((16,)), dma((24,)), dma((32,)), dma((2,)), dma((8,)), dma((8,)),
            dma((2,)), dma((2,)), dma, dma, dma((hops,)), dma((hops,)), dma((64,)), dma,
        ],
        compiler_params=pltpu.CompilerParams(
            collective_id=0, has_side_effects=True, vmem_limit_bytes=63 * 1024 * 1024
        ),
        name="stack",
    )(
        inputs, jnp.transpose(segments, (1, 2, 0)), norm_gains, w_query, w_keyval, w_output,
        jnp.asarray(np.stack(rope_tables())),
    )
    return out.reshape(MICRO, 1, 2, WIDTH)


def solution(mesh):
    return jax.shard_map(
        shards,
        mesh=mesh,
        in_specs=(
            P(None, "fsdp", "section", None),
            P(None, "fsdp", "section"),
            P("section", "fsdp"),
            P("section", "fsdp", None),
            P("section", "fsdp", None),
            P("section", "fsdp", None),
        ),
        out_specs=P(None, "fsdp", "section", None),
        check_vma=False,
    )
```
